32 devices in a mesh: dp: 4 (over y, x), frame: 8 (over z, core).
Axes of the slice: x: 2, y: 2, z: 4, core: 2. Of those that a mesh axis runs over, the one named last changes fastest.
Arguments:
- video: bfloat16 [4, 32, 8, 64, 256], P('dp', 'frame'), may hold values from -6 to 6
- saved: bfloat16 [4, 32, 8, 64, 256], P('dp', 'frame'), may hold values from -6 to 6
- grad_out: bfloat16 [4, 32, 8, 64, 256], P('dp', 'frame'), may hold values from -6 to 6
- spatial_w: bfloat16 [2304, 256], replicated, may hold values from -0.125 to 0.125
- temporal_w: bfloat16 [768, 256], replicated, may hold values from -0.21875 to 0.21875
Outputs:
- grad_video: bfloat16 [4, 32, 8, 64, 256], P('dp', 'frame')
- grad_spatial: float32 [2304, 256], P('frame', 'dp')
- grad_temporal: float32 [768, 256], P('frame', 'dp')
The draws below stay inside these ranges and needn't reach their ends.
All inputs are finite; a program needn't handle non-finite values.
Results may differ from the reference program's by a relative error of at most 0.0049.
Values may be sent and summed in bfloat16 or wider, within the bound.
A program may use at most 64 MiB of HBM per device.

```python
import math
import jax
import jax.numpy as jnp
from jax import lax

C = 256
KS = 9
KT = 3
HGT = 8
WID = 64
CLIPS = 4
FRAMES = 32


def level_of(rng, extent, split, low, largest):
    def one(dim, blocks):
        steps = jax.random.uniform(jax.random.fold_in(jax.random.fold_in(rng, 6), dim), (blocks,), jnp.float32, low / len(split), largest / len(split))
        return jnp.repeat(jnp.exp(steps), extent[dim] // blocks).reshape((-1,) + (1,) * (len(extent) - dim - 1))

    level = one(*split[0])
    for cut in split[1:]:
        level = level * one(*cut)
    return level


def bell_draw(rng, dims, deviation, bound, cuts=(), kind=jnp.bfloat16):
    drawn = jax.random.normal(rng, dims, jnp.float32) * deviation
    if len(cuts) > 0:
        drawn = level_of(rng, dims, cuts, -0.22, 0.18) * drawn
    return jnp.clip(drawn, min=-bound, max=bound).astype(kind)


def setup_inputs(seed: int = 0) -> dict:
    key_of = jax.random.split(jax.random.key(seed), 6)
    return {
        "video": bell_draw(key_of[0], (CLIPS, FRAMES, HGT, WID, C), 1.0, 6.0, ((0, 4), (1, 8))),
        "saved": bell_draw(key_of[1], (CLIPS, FRAMES, HGT, WID, C), 1.0, 6.0, ((0, 4), (1, 8))),
        "grad_out": bell_draw(key_of[2], (CLIPS, FRAMES, HGT, WID, C), 1.0, 6.0, ((0, 4), (1, 8))),
        "spatial_w": bell_draw(key_of[3], (KS * C, C), (KS * C) ** -0.5, 0.125),
        "temporal_w": bell_draw(key_of[4], (KT * C, C), (KT * C) ** -0.5, 0.21875),
    }


def shifted(source, row_off, col_off):
    height = source.shape[1]
    width = source.shape[2]
    padded = jnp.pad(source, ((0, 0), (1, 1), (1, 1), (0, 0)))
    return padded[:, 1 + row_off:1 + row_off + height, 1 + col_off:1 + col_off + width, :]

def temporal_back(grad_ext, saved_ext, frames, temporal_w, channels):
    lag_count = temporal_w.shape[0] // channels
    grad_now = grad_ext[:frames].reshape(-1, channels)
    hidden = jnp.zeros((grad_now.shape[0], channels), jnp.float32)
    blocks = []
    for lag in range(lag_count):
        weight_block = temporal_w[lag * channels:(lag + 1) * channels]
        later = grad_ext[lag:lag + frames].reshape(-1, channels)
        hidden = hidden + lax.dot_general(later, weight_block, (((1,), (1,)), ((), ())), preferred_element_type=jnp.float32)
        earlier = saved_ext[lag_count - 1 - lag:lag_count - 1 - lag + frames].reshape(-1, channels)
        blocks.append(lax.dot_general(earlier, grad_now, (((0,), (0,)), ((), ())), preferred_element_type=jnp.float32))
    return (hidden.astype(jnp.bfloat16), jnp.concatenate(blocks, axis=0))

def spatial_back(video_clip, grad_hidden, spatial_w, channels):
    grad_flat = grad_hidden.reshape(-1, channels)
    result = jnp.zeros(grad_flat.shape, jnp.float32)
    blocks = []
    for row_off in (-1, 0, 1):
        for col_off in (-1, 0, 1):
            tap_index = (row_off + 1) * 3 + (col_off + 1)
            weight_block = spatial_w[tap_index * channels:(tap_index + 1) * channels]
            moved = shifted(grad_hidden, -row_off, -col_off).reshape(-1, channels)
            result = result + lax.dot_general(moved, weight_block, (((1,), (1,)), ((), ())), preferred_element_type=jnp.float32)
            patch = shifted(video_clip, row_off, col_off).reshape(-1, channels)
            blocks.append(lax.dot_general(patch, grad_flat, (((0,), (0,)), ((), ())), preferred_element_type=jnp.float32))
    return (result.astype(jnp.bfloat16).reshape(grad_hidden.shape), jnp.concatenate(blocks, axis=0))

def reference(video, saved, grad_out, spatial_w, temporal_w):

    def one_clip(items):
        video_clip, saved_clip, grad_clip = items
        rim_zeros = jnp.zeros((KT - 1,) + grad_clip.shape[1:], jnp.bfloat16)
        grad_ext = jnp.concatenate([grad_clip, rim_zeros], axis=0)
        saved_ext = jnp.concatenate([rim_zeros, saved_clip], axis=0)
        hidden, wt_part = temporal_back(grad_ext, saved_ext, FRAMES, temporal_w, C)
        hidden = hidden.reshape(grad_clip.shape)
        grad_clip_in, ws_part = spatial_back(video_clip, hidden, spatial_w, C)
        return (grad_clip_in, ws_part, wt_part)
    grad_video, ws_parts, wt_parts = lax.map(one_clip, (video, saved, grad_out))
    factor = 1.0 / math.sqrt(float(CLIPS * FRAMES * HGT * WID))
    return (grad_video, lax.optimization_barrier(jnp.sum(ws_parts, axis=0)) * factor, lax.optimization_barrier(jnp.sum(wt_parts, axis=0)) * factor)
```

```python
import functools
import math

import jax
import jax.numpy as jnp
from jax import lax
from jax.experimental import pallas as pl
from jax.experimental.pallas import tpu as pltpu
from jax.sharding import PartitionSpec as P

F32 = jnp.float32
BF16 = jnp.bfloat16
MESH = pl.DeviceIdType.MESH
LANES = 128
CORES = 2


def nt(lhs, rhs):
    return lax.dot_general(lhs, rhs, (((1,), (1,)), ((), ())), preferred_element_type=F32)


def nn(lhs, rhs):
    return lax.dot_general(lhs, rhs, (((1,), (0,)), ((), ())), preferred_element_type=F32)


def kernel(
    nd, nf, width, factor,
    g_hbm, s_hbm, v_hbm, sw_hbm, tw_hbm,
    gv_hbm, ows, owt,
    gext, sv, vv, sw, tw, st, vt, hid, part, gv, s1, r1, s2, r2, s3, r3, own3,
    in_sem, out_sem, halo_send, halo_recv, send1, recv1, send2, recv2, send3, recv3,
):
    nz = nf // CORES
    frames, pixels, ch = v_hbm.shape
    lags = tw_hbm.shape[0] // ch
    taps = sw_hbm.shape[0] // ch
    rim = lags - 1
    early = frames - rim
    sw_rows = sw_hbm.shape[0]
    rw, rt = sw_rows // nf, tw_hbm.shape[0] // nf
    rows = rw + rt
    col = ch // nd
    fold = max(1, LANES // col)
    lane_w = col * fold
    prow = rows // fold

    di, fi = lax.axis_index("dp"), lax.axis_index("frame")
    core, zi = lax.rem(fi, CORES), fi // CORES
    mate = zi * CORES + (CORES - 1 - core)

    loads = []
    for i, (src, dst) in enumerate(
        ((g_hbm, gext.at[pl.ds(0, frames)]), (tw_hbm, tw), (s_hbm, sv), (v_hbm, vv), (sw_hbm, sw))
    ):
        copy = pltpu.make_async_copy(src, dst, in_sem.at[i])
        copy.start()
        loads.append(copy)

    barrier = pltpu.get_barrier_semaphore()
    greeted = [{"frame": mate}, {"frame": lax.rem(fi + 1, nf)}, {"frame": lax.rem(fi + nf - 1, nf)}]
    greeted += [{"dp": lax.rem(di + k, nd)} for k in range(1, nd)]
    greeted += [{"frame": lax.rem(zi + k, nz) * CORES + core} for k in range(1, nz)]
    for device in greeted:
        pl.semaphore_signal(barrier, inc=1, device_id=device, device_id_type=MESH)
    pl.semaphore_wait(barrier, len(greeted))

    halos = [
        pltpu.make_async_remote_copy(
            src_ref=g_hbm.at[i], dst_ref=gext.at[frames + i],
            send_sem=halo_send.at[i], recv_sem=halo_recv.at[i],
            device_id={"frame": lax.rem(fi + nf - 1, nf)}, device_id_type=MESH,
        )
        for i in range(rim)
    ]

    @pl.when(fi > 0)
    def _():
        for halo in halos:
            halo.start()

    @pl.when(fi == nf - 1)
    def _():
        gext[frames:] = jnp.zeros((rim, pixels, ch), BF16)

    blank = jnp.zeros((3, frames, width, ch), BF16)
    hid[:, :, :width] = blank
    hid[:, :, width + pixels:] = blank

    column = lax.rem(lax.broadcasted_iota(jnp.int32, (pixels, ch), 0), width)

    def hidden(s):
        later = jnp.concatenate([gext[s + k] for k in range(lags)], axis=1)
        weight = jnp.concatenate([tw[k * ch:(k + 1) * ch] for k in range(lags)], axis=1)
        value = nt(later, weight)
        for b in (-1, 0, 1):
            moved = value
            if b == 1:
                moved = jnp.where(column >= 1, pltpu.roll(value, 1, 0), 0.0)
            if b == -1:
                moved = jnp.where(column < width - 1, pltpu.roll(value, pixels - 1, 0), 0.0)
            hid[b + 1, s, width:width + pixels] = moved.astype(BF16)

    def moved_rows(a):
        return pl.ds(width - a * width, pixels)

    def grad_video(s):
        moved = jnp.concatenate(
            [hid[b + 1, s, moved_rows(a)] for a in (-1, 0, 1) for b in (-1, 0, 1)], axis=1
        )
        weight = jnp.concatenate([sw[t * ch:(t + 1) * ch] for t in range(taps)], axis=1)
        gv[s] = nt(moved, weight).astype(BF16)
        copy = pltpu.make_async_copy(gv.at[s], gv_hbm.at[s], out_sem.at[s])
        copy.start()
        return copy

    loads[0].wait()
    loads[1].wait()
    for s in range(early):
        hidden(s)
    loads[2].wait()
    for s in range(frames):
        st[:, s * pixels:(s + 1) * pixels] = sv[s].T
    for k in range(lags):
        part[sw_rows + k * ch:sw_rows + (k + 1) * ch] = nn(
            st[:, :(frames - k) * pixels], gext[k:frames].reshape(-1, ch)
        )
    loads[3].wait()
    for s in range(frames):
        vt[:, s * pixels:(s + 1) * pixels] = vv[s].T
    for a in (-1, 0, 1):
        for b in (-1, 0, 1):
            t = (a + 1) * 3 + b + 1
            part[t * ch:(t + 1) * ch] = nn(
                vt[:, :early * pixels],
                hid[b + 1, :early, width - a * width:width - a * width + pixels].reshape(-1, ch),
            )
    loads[4].wait()
    stores = [grad_video(s) for s in range(early)]

    for i in range(rim):
        @pl.when(fi < nf - 1)
        def _():
            halos[i].wait_recv()
        hidden(early + i)
    for k in range(1, lags):
        part[sw_rows + k * ch:sw_rows + (k + 1) * ch] += nn(
            st[:, (frames - k) * pixels:], gext[frames:frames + k].reshape(-1, ch)
        )

    def group_z(j):
        return lax.rem(zi + 1 + j, nz)

    def group_rows(j, owner_core):
        owner = group_z(j) * CORES + owner_core
        first = part[pl.ds(pl.multiple_of(owner * rw, math.gcd(rw, 256)), rw)]
        second = part[pl.ds(pl.multiple_of(sw_rows + owner * rt, math.gcd(rt, 256)), rt)]
        return jnp.concatenate([first, second], axis=0)

    def to_mate(j):
        s1[j] = group_rows(j, CORES - 1 - core).astype(BF16)
        copy = pltpu.make_async_remote_copy(
            src_ref=s1.at[j], dst_ref=r1.at[j], send_sem=send1.at[j], recv_sem=recv1.at[j],
            device_id={"frame": mate}, device_id_type=MESH,
        )
        copy.start()
        return copy

    start = group_z(0) * CORES * rw
    first_tap = start // ch
    lead = max((z * CORES * rw) % ch for z in range(nz))
    copies1 = []
    for i in range(taps):
        t = lax.rem(first_tap + i, taps)
        b = lax.rem(t, 3)
        top = pl.multiple_of(2 * width - (t // 3) * width, 16)
        spot = pl.ds(pl.multiple_of(t * ch, ch), ch)
        part[spot] += nn(
            vt[:, early * pixels:], hid[b, early:, pl.ds(top, pixels)].reshape(-1, ch)
        )
        while len(copies1) < nz and (
            i == taps - 1 or lead + (len(copies1) + 1) * CORES * rw <= (i + 1) * ch
        ):
            copies1.append(to_mate(len(copies1)))

    lane = lax.broadcasted_iota(jnp.int32, (prow, lane_w), 1)
    copies2 = []
    for j in range(nz):
        copies1[j].wait_recv()
        total = group_rows(j, core) + r1[j].astype(F32)
        for d in range(nd):
            tile, off = (d * col) // lane_w, (d * col) % lane_w
            piece = None
            for q in range(fold):
                block = total[q * prow:(q + 1) * prow, tile * lane_w:(tile + 1) * lane_w]
                turn = (q * col - off) % lane_w
                if turn:
                    block = pltpu.roll(block, turn, 1)
                piece = block if piece is None else jnp.where(lane >= q * col, block, piece)
            s2[d, j] = piece.astype(BF16)
        for k in range(1, nd):
            to = lax.rem(di + k, nd)
            copy = pltpu.make_async_remote_copy(
                src_ref=s2.at[to, j], dst_ref=r2.at[k - 1, j],
                send_sem=send2.at[k - 1, j], recv_sem=recv2.at[k - 1, j],
                device_id={"dp": to}, device_id_type=MESH,
            )
            copy.start()
            copies2.append(copy)

    stores += [grad_video(s) for s in range(early, frames)]

    copies3 = []
    for j in range(nz):
        for k in range(nd - 1):
            copies2[j * (nd - 1) + k].wait_recv()
        total = s2[di, j].astype(F32)
        for k in range(nd - 1):
            total = total + r2[k, j].astype(F32)
        if j == nz - 1:
            own3[...] = total
        else:
            s3[j] = total.astype(BF16)
            copy = pltpu.make_async_remote_copy(
                src_ref=s3.at[j], dst_ref=r3.at[j], send_sem=send3.at[j], recv_sem=recv3.at[j],
                device_id={"frame": group_z(j) * CORES + core}, device_id_type=MESH,
            )
            copy.start()
            copies3.append(copy)

    total = own3[...]
    for j in range(nz - 1):
        copies3[j].wait_recv()
        total = total + r3[j].astype(F32)
    total = total * factor
    total = jnp.concatenate([total[:, q * col:(q + 1) * col] for q in range(fold)], axis=0)
    ows[...] = total[:rw]
    owt[...] = total[rw:]

    for copy in stores:
        copy.wait()
    for copy in copies1 + copies2 + copies3:
        copy.wait_send()

    @pl.when(fi > 0)
    def _():
        for halo in halos:
            halo.wait_send()


def local(nd, nf, video, saved, grad_out, spatial_w, temporal_w):
    _, frames, height, width, ch = video.shape
    pixels = height * width
    nz = nf // CORES
    lags, taps = temporal_w.shape[0] // ch, spatial_w.shape[0] // ch
    rw, rt = spatial_w.shape[0] // nf, temporal_w.shape[0] // nf
    rows, col = rw + rt, ch // nd
    fold = max(1, LANES // col)
    prow, lane_w = rows // fold, col * fold
    slab = (frames, pixels, ch)
    factor = 1.0 / math.sqrt(float(nd * nf * frames * pixels))
    flops = 2 * frames * pixels * ch * ch * 2 * (lags + taps)
    anywhere = pl.BlockSpec(memory_space=pl.ANY)
    onchip = pl.BlockSpec(memory_space=pltpu.VMEM)
    dma = pltpu.SemaphoreType.DMA
    gv, gs, gt = pl.pallas_call(
        functools.partial(kernel, nd, nf, width, factor),
        out_shape=(
            jax.ShapeDtypeStruct(slab, BF16),
            jax.ShapeDtypeStruct((rw, col), F32),
            jax.ShapeDtypeStruct((rt, col), F32),
        ),
        in_specs=[anywhere] * 5,
        out_specs=(anywhere, onchip, onchip),
        scratch_shapes=[
            pltpu.VMEM((frames + lags - 1, pixels, ch), BF16),
            pltpu.VMEM(slab, BF16),
            pltpu.VMEM(slab, BF16),
            pltpu.VMEM(spatial_w.shape, BF16),
            pltpu.VMEM(temporal_w.shape, BF16),
            pltpu.VMEM((ch, frames * pixels), BF16),
            pltpu.VMEM((ch, frames * pixels), BF16),
            pltpu.VMEM((3, frames, pixels + 2 * width, ch), BF16),
            pltpu.VMEM((spatial_w.shape[0] + temporal_w.shape[0], ch), F32),
            pltpu.VMEM(slab, BF16),
            pltpu.VMEM((nz, rows, ch), BF16),
            pltpu.VMEM((nz, rows, ch), BF16),
            pltpu.VMEM((nd, nz, prow, lane_w), BF16),
            pltpu.VMEM((nd - 1, nz, prow, lane_w), BF16),
            pltpu.VMEM((nz - 1, prow, lane_w), BF16),
            pltpu.VMEM((nz - 1, prow, lane_w), BF16),
            pltpu.VMEM((prow, lane_w), F32),
            dma((5,)),
            dma((frames,)),
            dma((lags - 1,)),
            dma((lags - 1,)),
            dma((nz,)),
            dma((nz,)),
            dma((nd - 1, nz)),
            dma((nd - 1, nz)),
            dma((nz - 1,)),
            dma((nz - 1,)),
        ],
        compiler_params=pltpu.CompilerParams(
            collective_id=0, has_side_effects=True, vmem_limit_bytes=48 * 1024 * 1024
        ),
        cost_estimate=pl.CostEstimate(
            flops=flops, bytes_accessed=8 * frames * pixels * ch, transcendentals=0
        ),
        name="conv_backward",
    )(
        grad_out.reshape(slab), saved.reshape(slab), video.reshape(slab), spatial_w, temporal_w
    )
    return (gv.reshape(video.shape), gs, gt)


def solution(mesh):
    nd, nf = mesh.shape["dp"], mesh.shape["frame"]
    return jax.shard_map(
        functools.partial(local, nd, nf),
        mesh=mesh,
        in_specs=(
            P("dp", "frame", None, None, None),
            P("dp", "frame", None, None, None),
            P("dp", "frame", None, None, None),
            P(),
            P(),
        ),
        out_specs=(P("dp", "frame", None, None, None), P("frame", "dp"), P("frame", "dp")),
        check_vma=False,
    )
```

```python
import functools
import math

import jax
import jax.numpy as jnp
from jax import lax
from jax.experimental import pallas as pl
from jax.experimental.pallas import tpu as pltpu
from jax.sharding import PartitionSpec as P

F32 = jnp.float32
BF16 = jnp.bfloat16
MESH = pl.DeviceIdType.MESH
LANES = 128
CORES = 2
VMEM_BYTES = 60 * 1024 * 1024


def nn(lhs, rhs):
    return lax.dot_general(lhs, rhs, (((1,), (0,)), ((), ())), preferred_element_type=F32)


def kernel(
    nd, nf, width, factor,
    g_hbm, s_hbm, v_hbm, sw_hbm, tw_hbm,
    gv_hbm, ows, owt,
    gext, sv, vv, sw, tw, swt, twt, st, vt, hid, part, gv, s1, r1, s2, r2, s3, r3, own3,
    in_sem, out_sem, halo_send, halo_recv, send1, recv1, send2, recv2, send3, recv3,
):
    nz = nf // CORES
    frames, pixels, ch = v_hbm.shape
    lags = tw_hbm.shape[0] // ch
    taps = sw_hbm.shape[0] // ch
    rim = lags - 1
    early = frames - rim
    sw_rows = sw_hbm.shape[0]
    rw, rt = sw_rows // nf, tw_hbm.shape[0] // nf
    rows = rw + rt
    col = ch // nd
    fold = max(1, LANES // col)
    lane_w = col * fold
    prow = rows // fold

    di, fi = lax.axis_index("dp"), lax.axis_index("frame")
    core, zi = lax.rem(fi, CORES), fi // CORES
    mate = zi * CORES + (CORES - 1 - core)

    loads = []
    for i, (src, dst) in enumerate(
        ((g_hbm, gext.at[pl.ds(0, frames)]), (tw_hbm, tw), (s_hbm, sv), (v_hbm, vv), (sw_hbm, sw))
    ):
        copy = pltpu.make_async_copy(src, dst, in_sem.at[i])
        copy.start()
        loads.append(copy)

    barrier = pltpu.get_barrier_semaphore()
    greeted = [{"frame": mate}, {"frame": lax.rem(fi + 1, nf)}, {"frame": lax.rem(fi + nf - 1, nf)}]
    greeted += [{"dp": lax.rem(di + k, nd)} for k in range(1, nd)]
    greeted += [{"frame": lax.rem(zi + k, nz) * CORES + core} for k in range(1, nz)]
    for device in greeted:
        pl.semaphore_signal(barrier, inc=1, device_id=device, device_id_type=MESH)
    pl.semaphore_wait(barrier, len(greeted))

    halos = [
        pltpu.make_async_remote_copy(
            src_ref=g_hbm.at[i], dst_ref=gext.at[frames + i],
            send_sem=halo_send.at[i], recv_sem=halo_recv.at[i],
            device_id={"frame": lax.rem(fi + nf - 1, nf)}, device_id_type=MESH,
        )
        for i in range(rim)
    ]

    @pl.when(fi > 0)
    def _():
        for halo in halos:
            halo.start()

    @pl.when(fi == nf - 1)
    def _():
        gext[frames:] = jnp.zeros((rim, pixels, ch), BF16)

    blank = jnp.zeros((3, frames, width, ch), BF16)
    hid[:, :, :width] = blank
    hid[:, :, width + pixels:] = blank

    column = lax.rem(lax.broadcasted_iota(jnp.int32, (pixels, ch), 0), width)

    def hidden(s):
        later = jnp.concatenate([gext[s + k] for k in range(lags)], axis=1)
        value = nn(later, twt[...])
        for b in (-1, 0, 1):
            moved = value
            if b == 1:
                moved = jnp.where(column >= 1, pltpu.roll(value, 1, 0), 0.0)
            if b == -1:
                moved = jnp.where(column < width - 1, pltpu.roll(value, pixels - 1, 0), 0.0)
            hid[b + 1, s, width:width + pixels] = moved.astype(BF16)

    def moved_rows(a):
        return pl.ds(width - a * width, pixels)

    def grad_video(s):
        moved = jnp.concatenate(
            [hid[b + 1, s, moved_rows(a)] for a in (-1, 0, 1) for b in (-1, 0, 1)], axis=1
        )
        gv[s] = nn(moved, swt[...]).astype(BF16)
        copy = pltpu.make_async_copy(gv.at[s], gv_hbm.at[s], out_sem.at[s])
        copy.start()
        return copy

    def temporal_grad(k, first, last):
        return nn(
            st[:, first * pixels:last * pixels], gext[first + k:last + k].reshape(-1, ch)
        )

    def spatial_grad(b, top, first, last):
        return nn(
            vt[:, first * pixels:last * pixels],
            hid[b, first:last, pl.ds(top, pixels)].reshape(-1, ch),
        )

    def lag_rows(k):
        return pl.ds(sw_rows + k * ch, ch)

    loads[1].wait()
    for k in range(lags):
        twt[k * ch:(k + 1) * ch] = tw[k * ch:(k + 1) * ch].T
    loads[0].wait()
    for s in range(early):
        hidden(s)
    loads[2].wait()
    for s in range(frames):
        st[:, s * pixels:(s + 1) * pixels] = sv[s].T
    for k in range(lags):
        part[lag_rows(k)] = temporal_grad(k, 0, frames - k)
    loads[3].wait()
    for s in range(frames):
        vt[:, s * pixels:(s + 1) * pixels] = vv[s].T
    for t in range(taps):
        part[t * ch:(t + 1) * ch] = spatial_grad(t % 3, 2 * width - (t // 3) * width, 0, early)
    loads[4].wait()
    for t in range(taps):
        swt[t * ch:(t + 1) * ch] = sw[t * ch:(t + 1) * ch].T

    for i in range(rim):
        @pl.when(fi < nf - 1)
        def _():
            halos[i].wait_recv()
        hidden(early + i)
        for k in range(i + 1, lags):
            part[lag_rows(k)] += temporal_grad(k, frames + i - k, frames + i - k + 1)
        if i < rim - 1:
            for t in range(taps):
                part[t * ch:(t + 1) * ch] += spatial_grad(
                    t % 3, 2 * width - (t // 3) * width, early + i, early + i + 1
                )

    def group_z(j):
        return lax.rem(zi + 1 + j, nz)

    def group_rows(j, owner_core):
        owner = group_z(j) * CORES + owner_core
        first = part[pl.ds(pl.multiple_of(owner * rw, math.gcd(rw, 256)), rw)]
        second = part[pl.ds(pl.multiple_of(sw_rows + owner * rt, math.gcd(rt, 256)), rt)]
        return jnp.concatenate([first, second], axis=0)

    def to_mate(j):
        s1[j] = group_rows(j, CORES - 1 - core).astype(BF16)
        copy = pltpu.make_async_remote_copy(
            src_ref=s1.at[j], dst_ref=r1.at[j], send_sem=send1.at[j], recv_sem=recv1.at[j],
            device_id={"frame": mate}, device_id_type=MESH,
        )
        copy.start()
        return copy

    lane = lax.broadcasted_iota(jnp.int32, (prow, lane_w), 1)
    copies1, copies2, copies3, stores = [], [], [], []

    def to_clips(j):
        copies1[j].wait_recv()
        total = group_rows(j, core) + r1[j].astype(F32)
        for d in range(nd):
            tile, off = (d * col) // lane_w, (d * col) % lane_w
            piece = None
            for q in range(fold):
                block = total[q * prow:(q + 1) * prow, tile * lane_w:(tile + 1) * lane_w]
                turn = (q * col - off) % lane_w
                if turn:
                    block = pltpu.roll(block, turn, 1)
                piece = block if piece is None else jnp.where(lane >= q * col, block, piece)
            s2[d, j] = piece.astype(BF16)
        for k in range(1, nd):
            to = lax.rem(di + k, nd)
            copy = pltpu.make_async_remote_copy(
                src_ref=s2.at[to, j], dst_ref=r2.at[k - 1, j],
                send_sem=send2.at[k - 1, j], recv_sem=recv2.at[k - 1, j],
                device_id={"dp": to}, device_id_type=MESH,
            )
            copy.start()
            copies2.append(copy)

    def to_owner(j):
        for k in range(nd - 1):
            copies2[j * (nd - 1) + k].wait_recv()
        total = s2[di, j].astype(F32)
        for k in range(nd - 1):
            total = total + r2[k, j].astype(F32)
        if j == nz - 1:
            own3[...] = total
        else:
            s3[j] = total.astype(BF16)
            copy = pltpu.make_async_remote_copy(
                src_ref=s3.at[j], dst_ref=r3.at[j], send_sem=send3.at[j], recv_sem=recv3.at[j],
                device_id={"frame": group_z(j) * CORES + core}, device_id_type=MESH,
            )
            copy.start()
            copies3.append(copy)

    first_tap = group_z(0) * CORES * rw // ch
    lead = max((z * CORES * rw) % ch for z in range(nz))
    for i in range(taps):
        t = lax.rem(first_tap + i, taps)
        top = pl.multiple_of(2 * width - (t // 3) * width, 16)
        spot = pl.ds(pl.multiple_of(t * ch, ch), ch)
        part[spot] += spatial_grad(lax.rem(t, 3), top, frames - 1, frames)
        while len(copies1) < nz and (
            i == taps - 1 or lead + (len(copies1) + 1) * CORES * rw <= (i + 1) * ch
        ):
            copies1.append(to_mate(len(copies1)))
            if len(copies1) > 1:
                to_clips(len(copies1) - 2)
    stores.append(grad_video(0))
    to_clips(nz - 1)
    for j in range(nz):
        if j + 1 < frames:
            stores.append(grad_video(j + 1))
        to_owner(j)
    for s in range(nz + 1, frames):
        stores.append(grad_video(s))

    total = own3[...]
    for j in range(nz - 1):
        copies3[j].wait_recv()
        total = total + r3[j].astype(F32)
    total = total * factor
    total = jnp.concatenate([total[:, q * col:(q + 1) * col] for q in range(fold)], axis=0)
    ows[...] = total[:rw].T
    owt[...] = total[rw:].T

    for copy in stores:
        copy.wait()
    for copy in copies1 + copies2 + copies3:
        copy.wait_send()

    @pl.when(fi > 0)
    def _():
        for halo in halos:
            halo.wait_send()


def place(gv, gs, gt, gv_out, gs_out, gt_out, sem):
    copies = [
        pltpu.make_async_copy(src, dst, sem.at[i])
        for i, (src, dst) in enumerate(((gv, gv_out), (gs, gs_out), (gt, gt_out)))
    ]
    for copy in copies:
        copy.start()
    for copy in copies:
        copy.wait()


def local(nd, nf, video, saved, grad_out, spatial_w, temporal_w):
    _, frames, height, width, ch = video.shape
    pixels = height * width
    nz = nf // CORES
    lags, taps = temporal_w.shape[0] // ch, spatial_w.shape[0] // ch
    rw, rt = spatial_w.shape[0] // nf, temporal_w.shape[0] // nf
    rows, col = rw + rt, ch // nd
    fold = max(1, LANES // col)
    prow, lane_w = rows // fold, col * fold
    slab = (frames, pixels, ch)
    factor = 1.0 / math.sqrt(float(nd * nf * frames * pixels))
    flops = 2 * frames * pixels * ch * ch * 2 * (lags + taps)
    anywhere = pl.BlockSpec(memory_space=pl.ANY)
    onchip = pl.BlockSpec(memory_space=pltpu.VMEM)
    dma = pltpu.SemaphoreType.DMA
    gv, gs, gt = pl.pallas_call(
        functools.partial(kernel, nd, nf, width, factor),
        out_shape=(
            jax.ShapeDtypeStruct(slab, BF16),
            jax.ShapeDtypeStruct((col, rw), F32),
            jax.ShapeDtypeStruct((col, rt), F32),
        ),
        in_specs=[anywhere] * 5,
        out_specs=(anywhere, onchip, onchip),
        scratch_shapes=[
            pltpu.VMEM((frames + lags - 1, pixels, ch), BF16),
            pltpu.VMEM(slab, BF16),
            pltpu.VMEM(slab, BF16),
            pltpu.VMEM(spatial_w.shape, BF16),
            pltpu.VMEM(temporal_w.shape, BF16),
            pltpu.VMEM(spatial_w.shape, BF16),
            pltpu.VMEM(temporal_w.shape, BF16),
            pltpu.VMEM((ch, frames * pixels), BF16),
            pltpu.VMEM((ch, frames * pixels), BF16),
            pltpu.VMEM((3, frames, pixels + 2 * width, ch), BF16),
            pltpu.VMEM((spatial_w.shape[0] + temporal_w.shape[0], ch), F32),
            pltpu.VMEM(slab, BF16),
            pltpu.VMEM((nz, rows, ch), BF16),
            pltpu.VMEM((nz, rows, ch), BF16),
            pltpu.VMEM((nd, nz, prow, lane_w), BF16),
            pltpu.VMEM((nd - 1, nz, prow, lane_w), BF16),
            pltpu.VMEM((nz - 1, prow, lane_w), BF16),
            pltpu.VMEM((nz - 1, prow, lane_w), BF16),
            pltpu.VMEM((prow, lane_w), F32),
            dma((5,)),
            dma((frames,)),
            dma((lags - 1,)),
            dma((lags - 1,)),
            dma((nz,)),
            dma((nz,)),
            dma((nd - 1, nz)),
            dma((nd - 1, nz)),
            dma((nz - 1,)),
            dma((nz - 1,)),
        ],
        compiler_params=pltpu.CompilerParams(
            collective_id=0, has_side_effects=True, vmem_limit_bytes=VMEM_BYTES
        ),
        cost_estimate=pl.CostEstimate(
            flops=flops, bytes_accessed=8 * frames * pixels * ch, transcendentals=0
        ),
        name="conv_backward",
    )(
        grad_out.reshape(slab), saved.reshape(slab), video.reshape(slab), spatial_w, temporal_w
    )
    gv, gs, gt = pl.pallas_call(
        place,
        out_shape=tuple(jax.ShapeDtypeStruct(x.shape, x.dtype) for x in (gv, gs, gt)),
        in_specs=[anywhere] * 3,
        out_specs=(anywhere,) * 3,
        scratch_shapes=[dma((3,))],
        compiler_params=pltpu.CompilerParams(vmem_limit_bytes=VMEM_BYTES),
        name="place_results",
    )(gv, gs, gt)
    return (gv.reshape(video.shape), gs.T, gt.T)


def solution(mesh):
    nd, nf = mesh.shape["dp"], mesh.shape["frame"]
    return jax.shard_map(
        functools.partial(local, nd, nf),
        mesh=mesh,
        in_specs=(
            P("dp", "frame", None, None, None),
            P("dp", "frame", None, None, None),
            P("dp", "frame", None, None, None),
            P(),
            P(),
        ),
        out_specs=(P("dp", "frame", None, None, None), P("frame", "dp"), P("frame", "dp")),
        check_vma=False,
    )
```

```python
import functools
import math

import jax
import jax.numpy as jnp
from jax import lax
from jax.experimental import pallas as pl
from jax.experimental.pallas import tpu as pltpu
from jax.sharding import PartitionSpec as P

F32 = jnp.float32
BF16 = jnp.bfloat16
MESH = pl.DeviceIdType.MESH
LANES = 128
CORES = 2
VMEM_BYTES = 60 * 1024 * 1024


def nn(lhs, rhs):
    return lax.dot_general(lhs, rhs, (((1,), (0,)), ((), ())), preferred_element_type=F32)


def kernel(
    nd, nf, width, factor,
    g_hbm, s_hbm, v_hbm, sw_hbm, tw_hbm,
    gv_hbm, ows, owt,
    gext, sv, vv, sw, tw, swt, twt, st, vt, hid, part, gv, s1, r1, s2, r2, s4, r4, half2, s3, r3, own3,
    in_sem, out_sem, halo_send, halo_recv, send1, recv1, send2, recv2, send4, recv4, send3, recv3,
):
    nz = nf // CORES
    frames, pixels, ch = v_hbm.shape
    lags = tw_hbm.shape[0] // ch
    taps = sw_hbm.shape[0] // ch
    rim = lags - 1
    early = frames - rim
    sw_rows = sw_hbm.shape[0]
    rw, rt = sw_rows // nf, tw_hbm.shape[0] // nf
    rows = rw + rt
    col = ch // nd
    fold = max(1, LANES // col)
    lane_w = col * fold
    prow = rows // fold

    di, fi = lax.axis_index("dp"), lax.axis_index("frame")
    core, zi = lax.rem(fi, CORES), fi // CORES
    mate = zi * CORES + (CORES - 1 - core)

    loads = []
    for i, (src, dst) in enumerate(
        ((g_hbm, gext.at[pl.ds(0, frames)]), (tw_hbm, tw), (s_hbm, sv), (v_hbm, vv), (sw_hbm, sw))
    ):
        copy = pltpu.make_async_copy(src, dst, in_sem.at[i])
        copy.start()
        loads.append(copy)

    barrier = pltpu.get_barrier_semaphore()
    greeted = [{"frame": mate}, {"frame": lax.rem(fi + 1, nf)}, {"frame": lax.rem(fi + nf - 1, nf)}]
    greeted += [{"dp": lax.rem(di + k, nd)} for k in range(1, nd)]
    greeted += [{"frame": lax.rem(zi + k, nz) * CORES + core} for k in range(1, nz)]
    for device in greeted:
        pl.semaphore_signal(barrier, inc=1, device_id=device, device_id_type=MESH)
    pl.semaphore_wait(barrier, len(greeted))

    halos = [
        pltpu.make_async_remote_copy(
            src_ref=g_hbm.at[i], dst_ref=gext.at[frames + i],
            send_sem=halo_send.at[i], recv_sem=halo_recv.at[i],
            device_id={"frame": lax.rem(fi + nf - 1, nf)}, device_id_type=MESH,
        )
        for i in range(rim)
    ]

    @pl.when(fi > 0)
    def _():
        for halo in halos:
            halo.start()

    @pl.when(fi == nf - 1)
    def _():
        gext[frames:] = jnp.zeros((rim, pixels, ch), BF16)

    blank = jnp.zeros((3, frames, width, ch), BF16)
    hid[:, :, :width] = blank
    hid[:, :, width + pixels:] = blank

    column = lax.rem(lax.broadcasted_iota(jnp.int32, (pixels, ch), 0), width)

    def hidden(s):
        later = jnp.concatenate([gext[s + k] for k in range(lags)], axis=1)
        value = nn(later, twt[...])
        for b in (-1, 0, 1):
            moved = value
            if b == 1:
                moved = jnp.where(column >= 1, pltpu.roll(value, 1, 0), 0.0)
            if b == -1:
                moved = jnp.where(column < width - 1, pltpu.roll(value, pixels - 1, 0), 0.0)
            hid[b + 1, s, width:width + pixels] = moved.astype(BF16)

    def moved_rows(a):
        return pl.ds(width - a * width, pixels)

    def grad_video(s):
        moved = jnp.concatenate(
            [hid[b + 1, s, moved_rows(a)] for a in (-1, 0, 1) for b in (-1, 0, 1)], axis=1
        )
        gv[s] = nn(moved, swt[...]).astype(BF16)
        copy = pltpu.make_async_copy(gv.at[s], gv_hbm.at[s], out_sem.at[s])
        copy.start()
        return copy

    def temporal_grad(k, first, last):
        return nn(
            st[:, first * pixels:last * pixels], gext[first + k:last + k].reshape(-1, ch)
        )

    def spatial_grad(b, top, first, last):
        return nn(
            vt[:, first * pixels:last * pixels],
            hid[b, first:last, pl.ds(top, pixels)].reshape(-1, ch),
        )

    def lag_rows(k):
        return pl.ds(sw_rows + k * ch, ch)

    loads[1].wait()
    for k in range(lags):
        twt[k * ch:(k + 1) * ch] = tw[k * ch:(k + 1) * ch].T
    loads[0].wait()
    for s in range(early):
        hidden(s)
    loads[2].wait()
    for s in range(frames):
        st[:, s * pixels:(s + 1) * pixels] = sv[s].T
    for k in range(lags):
        part[lag_rows(k)] = temporal_grad(k, 0, frames - k)
    loads[3].wait()
    for s in range(frames):
        vt[:, s * pixels:(s + 1) * pixels] = vv[s].T
    for t in range(taps):
        part[t * ch:(t + 1) * ch] = spatial_grad(t % 3, 2 * width - (t // 3) * width, 0, early)
    for i in range(rim):
        @pl.when(fi < nf - 1)
        def _():
            halos[i].wait_recv()
        hidden(early + i)
        for k in range(i + 1, lags):
            part[lag_rows(k)] += temporal_grad(k, frames + i - k, frames + i - k + 1)
        if i < rim - 1:
            for t in range(taps):
                part[t * ch:(t + 1) * ch] += spatial_grad(
                    t % 3, 2 * width - (t // 3) * width, early + i, early + i + 1
                )

    def group_z(j):
        return lax.rem(zi + 1 + j, nz)

    def group_rows(j, owner_core):
        owner = group_z(j) * CORES + owner_core
        first = part[pl.ds(pl.multiple_of(owner * rw, math.gcd(rw, 256)), rw)]
        second = part[pl.ds(pl.multiple_of(sw_rows + owner * rt, math.gcd(rt, 256)), rt)]
        return jnp.concatenate([first, second], axis=0)

    def to_mate(j):
        s1[j] = group_rows(j, CORES - 1 - core).astype(BF16)
        copy = pltpu.make_async_remote_copy(
            src_ref=s1.at[j], dst_ref=r1.at[j], send_sem=send1.at[j], recv_sem=recv1.at[j],
            device_id={"frame": mate}, device_id_type=MESH,
        )
        copy.start()
        return copy

    lane = lax.broadcasted_iota(jnp.int32, (prow, lane_w), 1)
    copies1, copies2, copies3, copies4, stores = [], [], [], [], []

    low = min(n for n in range(1, nd + 1) if nd % n == 0 and n * n >= nd)
    high = nd // low
    dx, dy = lax.rem(di, low), di // low

    def split(j):
        if j % 2 == 0:
            return low, high, dx, dy
        return high, low, dy, dx

    def clip_device(j, a, b):
        return {"dp": b * low + a if j % 2 == 0 else a * low + b}

    def to_clips(j):
        copies1[j].wait_recv()
        na, nb, a, b = split(j)
        total = group_rows(j, core) + r1[j].astype(F32)
        for d in range(nd):
            tile, off = (d * col) // lane_w, (d * col) % lane_w
            piece = None
            for q in range(fold):
                block = total[q * prow:(q + 1) * prow, tile * lane_w:(tile + 1) * lane_w]
                turn = (q * col - off) % lane_w
                if turn:
                    block = pltpu.roll(block, turn, 1)
                piece = block if piece is None else jnp.where(lane >= q * col, block, piece)
            spot = (d % low) * high + d // low if j % 2 == 0 else d
            s2[j, spot] = piece.astype(BF16)
        sends = []
        for k in range(1, na):
            to = lax.rem(a + k, na)
            copy = pltpu.make_async_remote_copy(
                src_ref=s2.at[j, pl.ds(to * nb, nb)], dst_ref=r2.at[j, pl.ds((k - 1) * nb, nb)],
                send_sem=send2.at[k - 1, j], recv_sem=recv2.at[k - 1, j],
                device_id=clip_device(j, to, b), device_id_type=MESH,
            )
            copy.start()
            sends.append(copy)
        copies2.append(sends)

    def to_half(j):
        na, nb, a, b = split(j)
        for copy in copies2[j]:
            copy.wait_recv()

        def summed(i):
            total = s2[j, a * nb + i].astype(F32)
            for k in range(na - 1):
                total = total + r2[j, k * nb + i].astype(F32)
            return total

        half2[j] = summed(b)
        sends = []
        for k in range(1, nb):
            to = lax.rem(b + k, nb)
            s4[j, k - 1] = summed(to).astype(BF16)
            copy = pltpu.make_async_remote_copy(
                src_ref=s4.at[j, k - 1], dst_ref=r4.at[j, k - 1],
                send_sem=send4.at[k - 1, j], recv_sem=recv4.at[k - 1, j],
                device_id=clip_device(j, a, to), device_id_type=MESH,
            )
            copy.start()
            sends.append(copy)
        copies4.append(sends)

    def to_owner(j):
        total = half2[j]
        for k, copy in enumerate(copies4[j]):
            copy.wait_recv()
            total = total + r4[j, k].astype(F32)
        if j == nz - 1:
            own3[...] = total
        else:
            s3[j] = total.astype(BF16)
            copy = pltpu.make_async_remote_copy(
                src_ref=s3.at[j], dst_ref=r3.at[j], send_sem=send3.at[j], recv_sem=recv3.at[j],
                device_id={"frame": group_z(j) * CORES + core}, device_id_type=MESH,
            )
            copy.start()
            copies3.append(copy)

    first_tap = group_z(0) * CORES * rw // ch
    lead = max((z * CORES * rw) % ch for z in range(nz))
    for i in range(taps):
        t = lax.rem(first_tap + i, taps)
        top = pl.multiple_of(2 * width - (t // 3) * width, 16)
        spot = pl.ds(pl.multiple_of(t * ch, ch), ch)
        part[spot] += spatial_grad(lax.rem(t, 3), top, frames - 1, frames)
        while len(copies1) < nz and (
            i == taps - 1 or lead + (len(copies1) + 1) * CORES * rw <= (i + 1) * ch
        ):
            copies1.append(to_mate(len(copies1)))
            if len(copies1) > 1:
                to_clips(len(copies1) - 2)
    to_clips(nz - 1)
    loads[4].wait()
    for t in range(taps):
        swt[t * ch:(t + 1) * ch] = sw[t * ch:(t + 1) * ch].T
    stores.append(grad_video(0))
    for j in range(nz):
        to_half(j)
        if j + 1 < frames:
            stores.append(grad_video(j + 1))
        if j >= 2:
            to_owner(j - 2)
    for s in range(nz + 1, frames):
        stores.append(grad_video(s))
    for j in range(max(nz - 2, 0), nz):
        to_owner(j)

    total = own3[...]
    for j in range(nz - 1):
        copies3[j].wait_recv()
        total = total + r3[j].astype(F32)
    total = total * factor
    total = jnp.concatenate([total[:, q * col:(q + 1) * col] for q in range(fold)], axis=0)
    ows[...] = total[:rw].T
    owt[...] = total[rw:].T

    for copy in stores:
        copy.wait()
    for copy in sum(copies2 + copies4, copies1 + copies3):
        copy.wait_send()

    @pl.when(fi > 0)
    def _():
        for halo in halos:
            halo.wait_send()


def place(gv, gs, gt, gv_out, gs_out, gt_out, gv_held, gs_held, gt_held, in_sem, out_sem):
    frames = gv.shape[0]
    hops = [(gv.at[s], gv_held.at[s], gv_out.at[s]) for s in range(frames)]
    hops += [(gs, gs_held, gs_out), (gt, gt_held, gt_out)]
    inward = [pltpu.make_async_copy(a, b, in_sem.at[i]) for i, (a, b, _) in enumerate(hops)]
    outward = [pltpu.make_async_copy(b, c, out_sem.at[i]) for i, (_, b, c) in enumerate(hops)]
    for copy in inward:
        copy.start()
    for first, second in zip(inward, outward):
        first.wait()
        second.start()
    for copy in outward:
        copy.wait()


def local(nd, nf, video, saved, grad_out, spatial_w, temporal_w):
    _, frames, height, width, ch = video.shape
    pixels = height * width
    nz = nf // CORES
    lags, taps = temporal_w.shape[0] // ch, spatial_w.shape[0] // ch
    rw, rt = spatial_w.shape[0] // nf, temporal_w.shape[0] // nf
    rows, col = rw + rt, ch // nd
    fold = max(1, LANES // col)
    prow, lane_w = rows // fold, col * fold
    slab = (frames, pixels, ch)
    factor = 1.0 / math.sqrt(float(nd * nf * frames * pixels))
    flops = 2 * frames * pixels * ch * ch * 2 * (lags + taps)
    anywhere = pl.BlockSpec(memory_space=pl.ANY)
    onchip = pl.BlockSpec(memory_space=pltpu.VMEM)
    dma = pltpu.SemaphoreType.DMA
    gv, gs, gt = pl.pallas_call(
        functools.partial(kernel, nd, nf, width, factor),
        out_shape=(
            jax.ShapeDtypeStruct(slab, BF16),
            jax.ShapeDtypeStruct((col, rw), F32),
            jax.ShapeDtypeStruct((col, rt), F32),
        ),
        in_specs=[anywhere] * 5,
        out_specs=(anywhere, onchip, onchip),
        scratch_shapes=[
            pltpu.VMEM((frames + lags - 1, pixels, ch), BF16),
            pltpu.VMEM(slab, BF16),
            pltpu.VMEM(slab, BF16),
            pltpu.VMEM(spatial_w.shape, BF16),
            pltpu.VMEM(temporal_w.shape, BF16),
            pltpu.VMEM(spatial_w.shape, BF16),
            pltpu.VMEM(temporal_w.shape, BF16),
            pltpu.VMEM((ch, frames * pixels), BF16),
            pltpu.VMEM((ch, frames * pixels), BF16),
            pltpu.VMEM((3, frames, pixels + 2 * width, ch), BF16),
            pltpu.VMEM((spatial_w.shape[0] + temporal_w.shape[0], ch), F32),
            pltpu.VMEM(slab, BF16),
            pltpu.VMEM((nz, rows, ch), BF16),
            pltpu.VMEM((nz, rows, ch), BF16),
            pltpu.VMEM((nz, nd, prow, lane_w), BF16),
            pltpu.VMEM((nz, nd, prow, lane_w), BF16),
            pltpu.VMEM((nz, nd, prow, lane_w), BF16),
            pltpu.VMEM((nz, nd, prow, lane_w), BF16),
            pltpu.VMEM((nz, prow, lane_w), F32),
            pltpu.VMEM((nz - 1, prow, lane_w), BF16),
            pltpu.VMEM((nz - 1, prow, lane_w), BF16),
            pltpu.VMEM((prow, lane_w), F32),
            dma((5,)),
            dma((frames,)),
            dma((lags - 1,)),
            dma((lags - 1,)),
            dma((nz,)),
            dma((nz,)),
            dma((nd - 1, nz)),
            dma((nd - 1, nz)),
            dma((nd - 1, nz)),
            dma((nd - 1, nz)),
            dma((nz - 1,)),
            dma((nz - 1,)),
        ],
        compiler_params=pltpu.CompilerParams(
            collective_id=0, has_side_effects=True, vmem_limit_bytes=VMEM_BYTES
        ),
        cost_estimate=pl.CostEstimate(
            flops=flops, bytes_accessed=8 * frames * pixels * ch, transcendentals=0
        ),
        name="conv_backward",
    )(
        grad_out.reshape(slab), saved.reshape(slab), video.reshape(slab), spatial_w, temporal_w
    )
    gv, gs, gt = pl.pallas_call(
        place,
        out_shape=tuple(jax.ShapeDtypeStruct(x.shape, x.dtype) for x in (gv, gs, gt)),
        in_specs=[anywhere] * 3,
        out_specs=(anywhere,) * 3,
        scratch_shapes=[pltpu.VMEM(x.shape, x.dtype) for x in (gv, gs, gt)]
        + [dma((frames + 2,)), dma((frames + 2,))],
        compiler_params=pltpu.CompilerParams(vmem_limit_bytes=VMEM_BYTES),
        name="place_results",
    )(gv, gs, gt)
    return (gv.reshape(video.shape), gs.T, gt.T)


def solution(mesh):
    nd, nf = mesh.shape["dp"], mesh.shape["frame"]
    return jax.shard_map(
        functools.partial(local, nd, nf),
        mesh=mesh,
        in_specs=(
            P("dp", "frame", None, None, None),
            P("dp", "frame", None, None, None),
            P("dp", "frame", None, None, None),
            P(),
            P(),
        ),
        out_specs=(P("dp", "frame", None, None, None), P("frame", "dp"), P("frame", "dp")),
        check_vma=False,
    )
```

```python
import functools
import math

import jax
import jax.numpy as jnp
from jax import lax
from jax.experimental import pallas as pl
from jax.experimental.pallas import tpu as pltpu
from jax.sharding import PartitionSpec as P

F32 = jnp.float32
BF16 = jnp.bfloat16
MESH = pl.DeviceIdType.MESH
LANES = 128
CORES = 2
VMEM_BYTES = 60 * 1024 * 1024


def nn(lhs, rhs):
    return lax.dot_general(lhs, rhs, (((1,), (0,)), ((), ())), preferred_element_type=F32)


def kernel(
    nd, nf, width, factor,
    g_hbm, s_hbm, v_hbm, sw_hbm, tw_hbm,
    gv_hbm, ows, owt,
    gext, sv, vv, sw, tw, swt, twt, st, vt, hid, part, gv, s1, r1, s2, r2, s3, r3, own3, gs, gt,
    in_sem, out_sem, halo_send, halo_recv, send1, recv1, send2, recv2, send3, recv3,
):
    nz = nf // CORES
    frames, pixels, ch = v_hbm.shape
    lags = tw_hbm.shape[0] // ch
    taps = sw_hbm.shape[0] // ch
    rim = lags - 1
    early = frames - rim
    sw_rows = sw_hbm.shape[0]
    rw, rt = sw_rows // nf, tw_hbm.shape[0] // nf
    rows = rw + rt
    col = ch // nd
    fold = max(1, LANES // col)
    lane_w = col * fold
    prow = rows // fold

    di, fi = lax.axis_index("dp"), lax.axis_index("frame")
    core, zi = lax.rem(fi, CORES), fi // CORES
    mate = zi * CORES + (CORES - 1 - core)

    loads = []
    for i, (src, dst) in enumerate(
        ((g_hbm, gext.at[pl.ds(0, frames)]), (tw_hbm, tw), (s_hbm, sv), (v_hbm, vv), (sw_hbm, sw))
    ):
        copy = pltpu.make_async_copy(src, dst, in_sem.at[i])
        copy.start()
        loads.append(copy)

    barrier = pltpu.get_barrier_semaphore()
    greeted = [{"frame": mate}, {"frame": lax.rem(fi + 1, nf)}, {"frame": lax.rem(fi + nf - 1, nf)}]
    greeted += [{"dp": lax.rem(di + k, nd)} for k in range(1, nd)]
    greeted += [{"frame": lax.rem(zi + k, nz) * CORES + core} for k in range(1, nz)]
    for device in greeted:
        pl.semaphore_signal(barrier, inc=1, device_id=device, device_id_type=MESH)
    pl.semaphore_wait(barrier, len(greeted))

    halos = [
        pltpu.make_async_remote_copy(
            src_ref=g_hbm.at[i], dst_ref=gext.at[frames + i],
            send_sem=halo_send.at[i], recv_sem=halo_recv.at[i],
            device_id={"frame": lax.rem(fi + nf - 1, nf)}, device_id_type=MESH,
        )
        for i in range(rim)
    ]

    @pl.when(fi > 0)
    def _():
        for halo in halos:
            halo.start()

    @pl.when(fi == nf - 1)
    def _():
        gext[frames:] = jnp.zeros((rim, pixels, ch), BF16)

    blank = jnp.zeros((3, frames, width, ch), BF16)
    hid[:, :, :width] = blank
    hid[:, :, width + pixels:] = blank

    column = lax.rem(lax.broadcasted_iota(jnp.int32, (pixels, ch), 0), width)

    def hidden(s):
        later = jnp.concatenate([gext[s + k] for k in range(lags)], axis=1)
        value = nn(later, twt[...])
        for b in (-1, 0, 1):
            moved = value
            if b == 1:
                moved = jnp.where(column >= 1, pltpu.roll(value, 1, 0), 0.0)
            if b == -1:
                moved = jnp.where(column < width - 1, pltpu.roll(value, pixels - 1, 0), 0.0)
            hid[b + 1, s, width:width + pixels] = moved.astype(BF16)

    def moved_rows(a):
        return pl.ds(width - a * width, pixels)

    def grad_video(s):
        moved = jnp.concatenate(
            [hid[b + 1, s, moved_rows(a)] for a in (-1, 0, 1) for b in (-1, 0, 1)], axis=1
        )
        gv[s] = nn(moved, swt[...]).astype(BF16)
        pltpu.make_async_copy(gv.at[s], gv_hbm.at[s], out_sem.at[s]).start()

    def temporal_grad(k, first, last):
        return nn(
            st[:, first * pixels:last * pixels], gext[first + k:last + k].reshape(-1, ch)
        )

    def spatial_grad(b, top, first, last):
        return nn(
            vt[:, first * pixels:last * pixels],
            hid[b, first:last, pl.ds(top, pixels)].reshape(-1, ch),
        )

    def lag_rows(k):
        return pl.ds(sw_rows + k * ch, ch)

    loads[1].wait()
    for k in range(lags):
        twt[k * ch:(k + 1) * ch] = tw[k * ch:(k + 1) * ch].T
    def loop(first, last):
        return lambda body: lax.fori_loop(first, last, lambda i, _: (body(i), None)[1], None)

    def tap_rows(t):
        return pl.ds(pl.multiple_of(t * ch, ch), ch)

    def tap_top(t):
        return pl.multiple_of(2 * width - (t // 3) * width, 16)

    def frame_lanes(s):
        return pl.ds(pl.multiple_of(s * pixels, LANES), pixels)

    loads[0].wait()
    loop(0, early)(hidden)
    loads[2].wait()

    @loop(0, frames)
    def _(s):
        st[:, frame_lanes(s)] = sv[s].T

    for k in range(lags):
        part[lag_rows(k)] = temporal_grad(k, 0, frames - k)
    loads[3].wait()

    @loop(0, frames)
    def _(s):
        vt[:, frame_lanes(s)] = vv[s].T

    @loop(0, taps)
    def _(t):
        part[tap_rows(t)] = spatial_grad(lax.rem(t, 3), tap_top(t), 0, early)

    loads[4].wait()

    @loop(0, taps)
    def _(t):
        swt[tap_rows(t)] = sw[tap_rows(t)].T

    for i in range(rim):
        @pl.when(fi < nf - 1)
        def _():
            halos[i].wait_recv()
        hidden(early + i)
        for k in range(i + 1, lags):
            part[lag_rows(k)] += temporal_grad(k, frames + i - k, frames + i - k + 1)
        if i < rim - 1:
            @loop(0, taps)
            def _(t):
                part[tap_rows(t)] += spatial_grad(
                    lax.rem(t, 3), tap_top(t), early + i, early + i + 1
                )

    def group_z(j):
        return lax.rem(zi + 1 + j, nz)

    def group_rows(j, owner_core):
        owner = group_z(j) * CORES + owner_core
        first = part[pl.ds(pl.multiple_of(owner * rw, math.gcd(rw, 256)), rw)]
        second = part[pl.ds(pl.multiple_of(sw_rows + owner * rt, math.gcd(rt, 256)), rt)]
        return jnp.concatenate([first, second], axis=0)

    def to_mate(j):
        s1[j] = group_rows(j, CORES - 1 - core).astype(BF16)
        copy = pltpu.make_async_remote_copy(
            src_ref=s1.at[j], dst_ref=r1.at[j], send_sem=send1.at[j], recv_sem=recv1.at[j],
            device_id={"frame": mate}, device_id_type=MESH,
        )
        copy.start()
        return copy

    lane = lax.broadcasted_iota(jnp.int32, (prow, lane_w), 1)
    copies1, copies2, copies3, stores = [], [], [], []

    def to_clips(j):
        copies1[j].wait_recv()
        total = group_rows(j, core) + r1[j].astype(F32)
        for d in range(nd):
            tile, off = (d * col) // lane_w, (d * col) % lane_w
            piece = None
            for q in range(fold):
                block = total[q * prow:(q + 1) * prow, tile * lane_w:(tile + 1) * lane_w]
                turn = (q * col - off) % lane_w
                if turn:
                    block = pltpu.roll(block, turn, 1)
                piece = block if piece is None else jnp.where(lane >= q * col, block, piece)
            s2[d, j] = piece.astype(BF16)
        for k in range(1, nd):
            to = lax.rem(di + k, nd)
            copy = pltpu.make_async_remote_copy(
                src_ref=s2.at[to, j], dst_ref=r2.at[k - 1, j],
                send_sem=send2.at[k - 1, j], recv_sem=recv2.at[k - 1, j],
                device_id={"dp": to}, device_id_type=MESH,
            )
            copy.start()
            copies2.append(copy)

    def to_owner(j):
        for k in range(nd - 1):
            copies2[j * (nd - 1) + k].wait_recv()
        total = s2[di, j].astype(F32)
        for k in range(nd - 1):
            total = total + r2[k, j].astype(F32)
        if j == nz - 1:
            own3[...] = total
        else:
            s3[j] = total.astype(BF16)
            copy = pltpu.make_async_remote_copy(
                src_ref=s3.at[j], dst_ref=r3.at[j], send_sem=send3.at[j], recv_sem=recv3.at[j],
                device_id={"frame": group_z(j) * CORES + core}, device_id_type=MESH,
            )
            copy.start()
            copies3.append(copy)

    first_tap = group_z(0) * CORES * rw // ch
    lead = max((z * CORES * rw) % ch for z in range(nz))
    done = 0
    for j in range(nz):
        needed = -(-(lead + (j + 1) * CORES * rw) // ch)
        needed = taps if j == nz - 1 else min(taps, needed)

        @loop(done, needed)
        def _(i):
            t = lax.rem(first_tap + i, taps)
            part[tap_rows(t)] += spatial_grad(lax.rem(t, 3), tap_top(t), frames - 1, frames)

        done = needed
        copies1.append(to_mate(j))
        if j > 0:
            to_clips(j - 1)
    loop(0, early)(grad_video)
    to_clips(nz - 1)
    loop(early, frames)(grad_video)
    for j in range(nz):
        to_owner(j)
    for s in range(frames):
        stores.append(pltpu.make_async_copy(gv.at[s], gv_hbm.at[s], out_sem.at[s]))

    total = own3[...]
    for j in range(nz - 1):
        copies3[j].wait_recv()
        total = total + r3[j].astype(F32)
    total = total * factor
    total = jnp.concatenate([total[:, q * col:(q + 1) * col] for q in range(fold)], axis=0)
    gs[...] = total[:rw].T
    gt[...] = total[rw:].T
    for i, (src, dst) in enumerate(((gs, ows), (gt, owt))):
        copy = pltpu.make_async_copy(src, dst, out_sem.at[frames + i])
        copy.start()
        stores.append(copy)

    for copy in stores:
        copy.wait()
    for copy in copies1 + copies2 + copies3:
        copy.wait_send()

    @pl.when(fi > 0)
    def _():
        for halo in halos:
            halo.wait_send()


def place(gv, gs, gt, gv_out, gs_out, gt_out, gv_held, gs_held, gt_held, in_sem, out_sem):
    frames = gv.shape[0]
    hops = [(gv.at[s], gv_held.at[s], gv_out.at[s]) for s in range(frames)]
    hops += [(gs, gs_held, gs_out), (gt, gt_held, gt_out)]
    inward = [pltpu.make_async_copy(a, b, in_sem.at[i]) for i, (a, b, _) in enumerate(hops)]
    outward = [pltpu.make_async_copy(b, c, out_sem.at[i]) for i, (_, b, c) in enumerate(hops)]
    for copy in inward:
        copy.start()
    for first, second in zip(inward, outward):
        first.wait()
        second.start()
    for copy in outward:
        copy.wait()


def local(nd, nf, video, saved, grad_out, spatial_w, temporal_w):
    _, frames, height, width, ch = video.shape
    pixels = height * width
    nz = nf // CORES
    lags, taps = temporal_w.shape[0] // ch, spatial_w.shape[0] // ch
    rw, rt = spatial_w.shape[0] // nf, temporal_w.shape[0] // nf
    rows, col = rw + rt, ch // nd
    fold = max(1, LANES // col)
    prow, lane_w = rows // fold, col * fold
    slab = (frames, pixels, ch)
    factor = 1.0 / math.sqrt(float(nd * nf * frames * pixels))
    flops = 2 * frames * pixels * ch * ch * 2 * (lags + taps)
    anywhere = pl.BlockSpec(memory_space=pl.ANY)
    dma = pltpu.SemaphoreType.DMA
    gv, gs, gt = pl.pallas_call(
        functools.partial(kernel, nd, nf, width, factor),
        out_shape=(
            jax.ShapeDtypeStruct(slab, BF16),
            jax.ShapeDtypeStruct((col, rw), F32),
            jax.ShapeDtypeStruct((col, rt), F32),
        ),
        in_specs=[anywhere] * 5,
        out_specs=(anywhere,) * 3,
        scratch_shapes=[
            pltpu.VMEM((frames + lags - 1, pixels, ch), BF16),
            pltpu.VMEM(slab, BF16),
            pltpu.VMEM(slab, BF16),
            pltpu.VMEM(spatial_w.shape, BF16),
            pltpu.VMEM(temporal_w.shape, BF16),
            pltpu.VMEM(spatial_w.shape, BF16),
            pltpu.VMEM(temporal_w.shape, BF16),
            pltpu.VMEM((ch, frames * pixels), BF16),
            pltpu.VMEM((ch, frames * pixels), BF16),
            pltpu.VMEM((3, frames, pixels + 2 * width, ch), BF16),
            pltpu.VMEM((spatial_w.shape[0] + temporal_w.shape[0], ch), F32),
            pltpu.VMEM(slab, BF16),
            pltpu.VMEM((nz, rows, ch), BF16),
            pltpu.VMEM((nz, rows, ch), BF16),
            pltpu.VMEM((nd, nz, prow, lane_w), BF16),
            pltpu.VMEM((nd - 1, nz, prow, lane_w), BF16),
            pltpu.VMEM((nz - 1, prow, lane_w), BF16),
            pltpu.VMEM((nz - 1, prow, lane_w), BF16),
            pltpu.VMEM((prow, lane_w), F32),
            pltpu.VMEM((col, rw), F32),
            pltpu.VMEM((col, rt), F32),
            dma((5,)),
            dma((frames + 2,)),
            dma((lags - 1,)),
            dma((lags - 1,)),
            dma((nz,)),
            dma((nz,)),
            dma((nd - 1, nz)),
            dma((nd - 1, nz)),
            dma((nz - 1,)),
            dma((nz - 1,)),
        ],
        compiler_params=pltpu.CompilerParams(
            collective_id=0, has_side_effects=True, vmem_limit_bytes=VMEM_BYTES
        ),
        cost_estimate=pl.CostEstimate(
            flops=flops, bytes_accessed=8 * frames * pixels * ch, transcendentals=0
        ),
        name="conv_backward",
    )(
        grad_out.reshape(slab), saved.reshape(slab), video.reshape(slab), spatial_w, temporal_w
    )
    gv, gs, gt = pl.pallas_call(
        place,
        out_shape=tuple(jax.ShapeDtypeStruct(x.shape, x.dtype) for x in (gv, gs, gt)),
        in_specs=[anywhere] * 3,
        out_specs=(anywhere,) * 3,
        scratch_shapes=[pltpu.VMEM(x.shape, x.dtype) for x in (gv, gs, gt)]
        + [dma((frames + 2,)), dma((frames + 2,))],
        compiler_params=pltpu.CompilerParams(vmem_limit_bytes=VMEM_BYTES),
        name="place_results",
    )(gv, gs, gt)
    return (gv.reshape(video.shape), gs.T, gt.T)


def solution(mesh):
    nd, nf = mesh.shape["dp"], mesh.shape["frame"]
    return jax.shard_map(
        functools.partial(local, nd, nf),
        mesh=mesh,
        in_specs=(
            P("dp", "frame", None, None, None),
            P("dp", "frame", None, None, None),
            P("dp", "frame", None, None, None),
            P(),
            P(),
        ),
        out_specs=(P("dp", "frame", None, None, None), P("frame", "dp"), P("frame", "dp")),
        check_vma=False,
    )
```

```python
import functools
import math

import jax
import jax.numpy as jnp
from jax import lax
from jax.experimental import pallas as pl
from jax.experimental.pallas import tpu as pltpu
from jax.sharding import PartitionSpec as P

F32 = jnp.float32
BF16 = jnp.bfloat16
MESH = pl.DeviceIdType.MESH
LANES = 128
CORES = 2
VMEM_BYTES = 60 * 1024 * 1024


def nn(lhs, rhs):
    return lax.dot_general(lhs, rhs, (((1,), (0,)), ((), ())), preferred_element_type=F32)


def kernel(
    nd, nf, width, factor,
    g_hbm, s_hbm, v_hbm, sw_hbm, tw_hbm,
    gv_hbm, ows, owt,
    gext, sv, vv, sw, tw, swt, twt, st, vt, hid, part, gv, s1, r1, s2, r2, s4, r4, half2, s3, r3, own3,
    in_sem, out_sem, halo_send, halo_recv, send1, recv1, send2, recv2, send4, recv4, send3, recv3,
):
    nz = nf // CORES
    frames, pixels, ch = v_hbm.shape
    lags = tw_hbm.shape[0] // ch
    taps = sw_hbm.shape[0] // ch
    rim = lags - 1
    early = frames - rim
    sw_rows = sw_hbm.shape[0]
    rw, rt = sw_rows // nf, tw_hbm.shape[0] // nf
    rows = rw + rt
    col = ch // nd
    fold = max(1, LANES // col)
    lane_w = col * fold
    prow = rows // fold

    di, fi = lax.axis_index("dp"), lax.axis_index("frame")
    core, zi = lax.rem(fi, CORES), fi // CORES
    mate = zi * CORES + (CORES - 1 - core)

    loads = []
    for i, (src, dst) in enumerate(
        ((g_hbm, gext.at[pl.ds(0, frames)]), (tw_hbm, tw), (s_hbm, sv), (v_hbm, vv), (sw_hbm, sw))
    ):
        copy = pltpu.make_async_copy(src, dst, in_sem.at[i])
        copy.start()
        loads.append(copy)

    barrier = pltpu.get_barrier_semaphore()
    greeted = [{"frame": mate}, {"frame": lax.rem(fi + 1, nf)}, {"frame": lax.rem(fi + nf - 1, nf)}]
    greeted += [{"dp": lax.rem(di + k, nd)} for k in range(1, nd)]
    greeted += [{"frame": lax.rem(zi + k, nz) * CORES + core} for k in range(1, nz)]
    for device in greeted:
        pl.semaphore_signal(barrier, inc=1, device_id=device, device_id_type=MESH)
    pl.semaphore_wait(barrier, len(greeted))

    halos = [
        pltpu.make_async_remote_copy(
            src_ref=g_hbm.at[i], dst_ref=gext.at[frames + i],
            send_sem=halo_send.at[i], recv_sem=halo_recv.at[i],
            device_id={"frame": lax.rem(fi + nf - 1, nf)}, device_id_type=MESH,
        )
        for i in range(rim)
    ]

    @pl.when(fi > 0)
    def _():
        for halo in halos:
            halo.start()

    @pl.when(fi == nf - 1)
    def _():
        gext[frames:] = jnp.zeros((rim, pixels, ch), BF16)

    blank = jnp.zeros((3, frames, width, ch), BF16)
    hid[:, :, :width] = blank
    hid[:, :, width + pixels:] = blank

    column = lax.rem(lax.broadcasted_iota(jnp.int32, (pixels, ch), 0), width)

    def hidden(s):
        later = jnp.concatenate([gext[s + k] for k in range(lags)], axis=1)
        value = nn(later, twt[...])
        for b in (-1, 0, 1):
            moved = value
            if b == 1:
                moved = jnp.where(column >= 1, pltpu.roll(value, 1, 0), 0.0)
            if b == -1:
                moved = jnp.where(column < width - 1, pltpu.roll(value, pixels - 1, 0), 0.0)
            hid[b + 1, s, width:width + pixels] = moved.astype(BF16)

    def moved_rows(a):
        return pl.ds(width - a * width, pixels)

    def grad_video(s):
        moved = jnp.concatenate(
            [hid[b + 1, s, moved_rows(a)] for a in (-1, 0, 1) for b in (-1, 0, 1)], axis=1
        )
        gv[s] = nn(moved, swt[...]).astype(BF16)
        copy = pltpu.make_async_copy(gv.at[s], gv_hbm.at[s], out_sem.at[s])
        copy.start()
        return copy

    def temporal_grad(k, first, last):
        return nn(
            st[:, first * pixels:last * pixels], gext[first + k:last + k].reshape(-1, ch)
        )

    def spatial_grad(b, top, first, last):
        return nn(
            vt[:, first * pixels:last * pixels],
            hid[b, first:last, pl.ds(top, pixels)].reshape(-1, ch),
        )

    def lag_rows(k):
        return pl.ds(sw_rows + k * ch, ch)

    loads[1].wait()
    for k in range(lags):
        twt[k * ch:(k + 1) * ch] = tw[k * ch:(k + 1) * ch].T
    loads[0].wait()
    for s in range(early):
        hidden(s)
    loads[2].wait()
    for s in range(frames):
        st[:, s * pixels:(s + 1) * pixels] = sv[s].T
    for k in range(lags):
        part[lag_rows(k)] = temporal_grad(k, 0, frames - k)
    loads[3].wait()
    for s in range(frames):
        vt[:, s * pixels:(s + 1) * pixels] = vv[s].T
    for t in range(taps):
        part[t * ch:(t + 1) * ch] = spatial_grad(t % 3, 2 * width - (t // 3) * width, 0, early)
    loads[4].wait()
    for t in range(taps):
        swt[t * ch:(t + 1) * ch] = sw[t * ch:(t + 1) * ch].T
    for i in range(rim):
        @pl.when(fi < nf - 1)
        def _():
            halos[i].wait_recv()
        hidden(early + i)
        for k in range(i + 1, lags):
            part[lag_rows(k)] += temporal_grad(k, frames + i - k, frames + i - k + 1)
        if i < rim - 1:
            for t in range(taps):
                part[t * ch:(t + 1) * ch] += spatial_grad(
                    t % 3, 2 * width - (t // 3) * width, early + i, early + i + 1
                )

    def group_z(j):
        return lax.rem(zi + 1 + j, nz)

    def group_rows(j, owner_core):
        owner = group_z(j) * CORES + owner_core
        first = part[pl.ds(pl.multiple_of(owner * rw, math.gcd(rw, 256)), rw)]
        second = part[pl.ds(pl.multiple_of(sw_rows + owner * rt, math.gcd(rt, 256)), rt)]
        return jnp.concatenate([first, second], axis=0)

    def to_mate(j):
        s1[j] = group_rows(j, CORES - 1 - core).astype(BF16)
        copy = pltpu.make_async_remote_copy(
            src_ref=s1.at[j], dst_ref=r1.at[j], send_sem=send1.at[j], recv_sem=recv1.at[j],
            device_id={"frame": mate}, device_id_type=MESH,
        )
        copy.start()
        return copy

    lane = lax.broadcasted_iota(jnp.int32, (prow, lane_w), 1)
    copies1, copies2, copies3, copies4, stores = [], [], [], [], []

    low = min(n for n in range(1, nd + 1) if nd % n == 0 and n * n >= nd)
    high = nd // low
    dx, dy = lax.rem(di, low), di // low

    def split(j):
        if j % 2 == 0:
            return low, high, dx, dy
        return high, low, dy, dx

    def clip_device(j, a, b):
        return {"dp": b * low + a if j % 2 == 0 else a * low + b}

    def to_clips(j):
        copies1[j].wait_recv()
        na, nb, a, b = split(j)
        total = group_rows(j, core) + r1[j].astype(F32)
        for d in range(nd):
            tile, off = (d * col) // lane_w, (d * col) % lane_w
            piece = None
            for q in range(fold):
                block = total[q * prow:(q + 1) * prow, tile * lane_w:(tile + 1) * lane_w]
                turn = (q * col - off) % lane_w
                if turn:
                    block = pltpu.roll(block, turn, 1)
                piece = block if piece is None else jnp.where(lane >= q * col, block, piece)
            spot = (d % low) * high + d // low if j % 2 == 0 else d
            s2[j, spot] = piece.astype(BF16)
        sends = []
        for k in range(1, na):
            to = lax.rem(a + k, na)
            copy = pltpu.make_async_remote_copy(
                src_ref=s2.at[j, pl.ds(to * nb, nb)], dst_ref=r2.at[j, pl.ds((k - 1) * nb, nb)],
                send_sem=send2.at[k - 1, j], recv_sem=recv2.at[k - 1, j],
                device_id=clip_device(j, to, b), device_id_type=MESH,
            )
            copy.start()
            sends.append(copy)
        copies2.append(sends)

    def to_half(j):
        na, nb, a, b = split(j)
        for copy in copies2[j]:
            copy.wait_recv()

        def summed(i):
            total = s2[j, a * nb + i].astype(F32)
            for k in range(na - 1):
                total = total + r2[j, k * nb + i].astype(F32)
            return total

        half2[j] = summed(b)
        sends = []
        for k in range(1, nb):
            to = lax.rem(b + k, nb)
            s4[j, k - 1] = summed(to).astype(BF16)
            copy = pltpu.make_async_remote_copy(
                src_ref=s4.at[j, k - 1], dst_ref=r4.at[j, k - 1],
                send_sem=send4.at[k - 1, j], recv_sem=recv4.at[k - 1, j],
                device_id=clip_device(j, a, to), device_id_type=MESH,
            )
            copy.start()
            sends.append(copy)
        copies4.append(sends)

    def to_owner(j):
        total = half2[j]
        for k, copy in enumerate(copies4[j]):
            copy.wait_recv()
            total = total + r4[j, k].astype(F32)
        if j == nz - 1:
            own3[...] = total
        else:
            s3[j] = total.astype(BF16)
            copy = pltpu.make_async_remote_copy(
                src_ref=s3.at[j], dst_ref=r3.at[j], send_sem=send3.at[j], recv_sem=recv3.at[j],
                device_id={"frame": group_z(j) * CORES + core}, device_id_type=MESH,
            )
            copy.start()
            copies3.append(copy)

    first_tap = group_z(0) * CORES * rw // ch
    lead = max((z * CORES * rw) % ch for z in range(nz))
    for i in range(taps):
        t = lax.rem(first_tap + i, taps)
        top = pl.multiple_of(2 * width - (t // 3) * width, 16)
        spot = pl.ds(pl.multiple_of(t * ch, ch), ch)
        part[spot] += spatial_grad(lax.rem(t, 3), top, frames - 1, frames)
        while len(copies1) < nz and (
            i == taps - 1 or lead + (len(copies1) + 1) * CORES * rw <= (i + 1) * ch
        ):
            copies1.append(to_mate(len(copies1)))
            if len(copies1) > 1:
                to_clips(len(copies1) - 2)
    stores.append(grad_video(0))
    to_clips(nz - 1)
    for j in range(nz):
        to_half(j)
        if j > 0:
            to_owner(j - 1)
        if j + 1 < frames:
            stores.append(grad_video(j + 1))
    for s in range(nz + 1, frames):
        stores.append(grad_video(s))
    to_owner(nz - 1)

    total = own3[...]
    for j in range(nz - 1):
        copies3[j].wait_recv()
        total = total + r3[j].astype(F32)
    total = total * factor
    total = jnp.concatenate([total[:, q * col:(q + 1) * col] for q in range(fold)], axis=0)
    ows[...] = total[:rw].T
    owt[...] = total[rw:].T

    for copy in stores:
        copy.wait()
    for copy in sum(copies2 + copies4, copies1 + copies3):
        copy.wait_send()

    @pl.when(fi > 0)
    def _():
        for halo in halos:
            halo.wait_send()


def place(gv, gs, gt, gv_out, gs_out, gt_out, gv_held, gs_held, gt_held, in_sem, out_sem):
    frames = gv.shape[0]
    hops = [(gv.at[s], gv_held.at[s], gv_out.at[s]) for s in range(frames)]
    hops += [(gs, gs_held, gs_out), (gt, gt_held, gt_out)]
    inward = [pltpu.make_async_copy(a, b, in_sem.at[i]) for i, (a, b, _) in enumerate(hops)]
    outward = [pltpu.make_async_copy(b, c, out_sem.at[i]) for i, (_, b, c) in enumerate(hops)]
    for copy in inward:
        copy.start()
    for first, second in zip(inward, outward):
        first.wait()
        second.start()
    for copy in outward:
        copy.wait()


def local(nd, nf, video, saved, grad_out, spatial_w, temporal_w):
    _, frames, height, width, ch = video.shape
    pixels = height * width
    nz = nf // CORES
    lags, taps = temporal_w.shape[0] // ch, spatial_w.shape[0] // ch
    rw, rt = spatial_w.shape[0] // nf, temporal_w.shape[0] // nf
    rows, col = rw + rt, ch // nd
    fold = max(1, LANES // col)
    prow, lane_w = rows // fold, col * fold
    slab = (frames, pixels, ch)
    factor = 1.0 / math.sqrt(float(nd * nf * frames * pixels))
    flops = 2 * frames * pixels * ch * ch * 2 * (lags + taps)
    anywhere = pl.BlockSpec(memory_space=pl.ANY)
    onchip = pl.BlockSpec(memory_space=pltpu.VMEM)
    dma = pltpu.SemaphoreType.DMA
    gv, gs, gt = pl.pallas_call(
        functools.partial(kernel, nd, nf, width, factor),
        out_shape=(
            jax.ShapeDtypeStruct(slab, BF16),
            jax.ShapeDtypeStruct((col, rw), F32),
            jax.ShapeDtypeStruct((col, rt), F32),
        ),
        in_specs=[anywhere] * 5,
        out_specs=(anywhere, onchip, onchip),
        scratch_shapes=[
            pltpu.VMEM((frames + lags - 1, pixels, ch), BF16),
            pltpu.VMEM(slab, BF16),
            pltpu.VMEM(slab, BF16),
            pltpu.VMEM(spatial_w.shape, BF16),
            pltpu.VMEM(temporal_w.shape, BF16),
            pltpu.VMEM(spatial_w.shape, BF16),
            pltpu.VMEM(temporal_w.shape, BF16),
            pltpu.VMEM((ch, frames * pixels), BF16),
            pltpu.VMEM((ch, frames * pixels), BF16),
            pltpu.VMEM((3, frames, pixels + 2 * width, ch), BF16),
            pltpu.VMEM((spatial_w.shape[0] + temporal_w.shape[0], ch), F32),
            pltpu.VMEM(slab, BF16),
            pltpu.VMEM((nz, rows, ch), BF16),
            pltpu.VMEM((nz, rows, ch), BF16),
            pltpu.VMEM((nz, nd, prow, lane_w), BF16),
            pltpu.VMEM((nz, nd, prow, lane_w), BF16),
            pltpu.VMEM((nz, nd, prow, lane_w), BF16),
            pltpu.VMEM((nz, nd, prow, lane_w), BF16),
            pltpu.VMEM((nz, prow, lane_w), F32),
            pltpu.VMEM((nz - 1, prow, lane_w), BF16),
            pltpu.VMEM((nz - 1, prow, lane_w), BF16),
            pltpu.VMEM((prow, lane_w), F32),
            dma((5,)),
            dma((frames,)),
            dma((lags - 1,)),
            dma((lags - 1,)),
            dma((nz,)),
            dma((nz,)),
            dma((nd - 1, nz)),
            dma((nd - 1, nz)),
            dma((nd - 1, nz)),
            dma((nd - 1, nz)),
            dma((nz - 1,)),
            dma((nz - 1,)),
        ],
        compiler_params=pltpu.CompilerParams(
            collective_id=0, has_side_effects=True, vmem_limit_bytes=VMEM_BYTES
        ),
        cost_estimate=pl.CostEstimate(
            flops=flops, bytes_accessed=8 * frames * pixels * ch, transcendentals=0
        ),
        name="conv_backward",
    )(
        grad_out.reshape(slab), saved.reshape(slab), video.reshape(slab), spatial_w, temporal_w
    )
    gv, gs, gt = pl.pallas_call(
        place,
        out_shape=tuple(jax.ShapeDtypeStruct(x.shape, x.dtype) for x in (gv, gs, gt)),
        in_specs=[anywhere] * 3,
        out_specs=(anywhere,) * 3,
        scratch_shapes=[pltpu.VMEM(x.shape, x.dtype) for x in (gv, gs, gt)]
        + [dma((frames + 2,)), dma((frames + 2,))],
        compiler_params=pltpu.CompilerParams(vmem_limit_bytes=VMEM_BYTES),
        name="place_results",
    )(gv, gs, gt)
    return (gv.reshape(video.shape), gs.T, gt.T)


def solution(mesh):
    nd, nf = mesh.shape["dp"], mesh.shape["frame"]
    return jax.shard_map(
        functools.partial(local, nd, nf),
        mesh=mesh,
        in_specs=(
            P("dp", "frame", None, None, None),
            P("dp", "frame", None, None, None),
            P("dp", "frame", None, None, None),
            P(),
            P(),
        ),
        out_specs=(P("dp", "frame", None, None, None), P("frame", "dp"), P("frame", "dp")),
        check_vma=False,
    )
```

```python
import functools
import math

import jax
import jax.numpy as jnp
from jax import lax
from jax.experimental import pallas as pl
from jax.experimental.pallas import tpu as pltpu
from jax.sharding import PartitionSpec as P

F32 = jnp.float32
BF16 = jnp.bfloat16
MESH = pl.DeviceIdType.MESH
LANES = 128
CORES = 2
VMEM_BYTES = 60 * 1024 * 1024


def nt(lhs, rhs):
    return lax.dot_general(lhs, rhs, (((1,), (1,)), ((), ())), preferred_element_type=F32)


def nn(lhs, rhs):
    return lax.dot_general(lhs, rhs, (((1,), (0,)), ((), ())), preferred_element_type=F32)


def kernel(
    nd, nf, width, factor,
    g_hbm, s_hbm, v_hbm, sw_hbm, tw_hbm,
    gv_hbm, ows, owt,
    gext, sv, vv, sw, tw, st, vt, hid, part, gv, s1, r1, s2, r2, s3, r3, own3,
    in_sem, out_sem, halo_send, halo_recv, send1, recv1, send2, recv2, send3, recv3,
):
    nz = nf // CORES
    frames, pixels, ch = v_hbm.shape
    lags = tw_hbm.shape[0] // ch
    taps = sw_hbm.shape[0] // ch
    rim = lags - 1
    early = frames - rim
    sw_rows = sw_hbm.shape[0]
    rw, rt = sw_rows // nf, tw_hbm.shape[0] // nf
    rows = rw + rt
    col = ch // nd
    fold = max(1, LANES // col)
    lane_w = col * fold
    prow = rows // fold

    di, fi = lax.axis_index("dp"), lax.axis_index("frame")
    core, zi = lax.rem(fi, CORES), fi // CORES
    mate = zi * CORES + (CORES - 1 - core)

    loads = []
    for i, (src, dst) in enumerate(
        ((g_hbm, gext.at[pl.ds(0, frames)]), (tw_hbm, tw), (s_hbm, sv), (v_hbm, vv), (sw_hbm, sw))
    ):
        copy = pltpu.make_async_copy(src, dst, in_sem.at[i])
        copy.start()
        loads.append(copy)

    barrier = pltpu.get_barrier_semaphore()
    greeted = [{"frame": mate}, {"frame": lax.rem(fi + 1, nf)}, {"frame": lax.rem(fi + nf - 1, nf)}]
    greeted += [{"dp": lax.rem(di + k, nd)} for k in range(1, nd)]
    greeted += [{"frame": lax.rem(zi + k, nz) * CORES + core} for k in range(1, nz)]
    for device in greeted:
        pl.semaphore_signal(barrier, inc=1, device_id=device, device_id_type=MESH)
    pl.semaphore_wait(barrier, len(greeted))

    halos = [
        pltpu.make_async_remote_copy(
            src_ref=g_hbm.at[i], dst_ref=gext.at[frames + i],
            send_sem=halo_send.at[i], recv_sem=halo_recv.at[i],
            device_id={"frame": lax.rem(fi + nf - 1, nf)}, device_id_type=MESH,
        )
        for i in range(rim)
    ]

    @pl.when(fi > 0)
    def _():
        for halo in halos:
            halo.start()

    @pl.when(fi == nf - 1)
    def _():
        gext[frames:] = jnp.zeros((rim, pixels, ch), BF16)

    blank = jnp.zeros((3, frames, width, ch), BF16)
    hid[:, :, :width] = blank
    hid[:, :, width + pixels:] = blank

    column = lax.rem(lax.broadcasted_iota(jnp.int32, (pixels, ch), 0), width)

    def hidden(s):
        later = jnp.concatenate([gext[s + k] for k in range(lags)], axis=1)
        weight = jnp.concatenate([tw[k * ch:(k + 1) * ch] for k in range(lags)], axis=1)
        value = nt(later, weight)
        for b in (-1, 0, 1):
            moved = value
            if b == 1:
                moved = jnp.where(column >= 1, pltpu.roll(value, 1, 0), 0.0)
            if b == -1:
                moved = jnp.where(column < width - 1, pltpu.roll(value, pixels - 1, 0), 0.0)
            hid[b + 1, s, width:width + pixels] = moved.astype(BF16)

    def moved_rows(a):
        return pl.ds(width - a * width, pixels)

    def grad_video(s):
        moved = jnp.concatenate(
            [hid[b + 1, s, moved_rows(a)] for a in (-1, 0, 1) for b in (-1, 0, 1)], axis=1
        )
        weight = jnp.concatenate([sw[t * ch:(t + 1) * ch] for t in range(taps)], axis=1)
        gv[s] = nt(moved, weight).astype(BF16)
        copy = pltpu.make_async_copy(gv.at[s], gv_hbm.at[s], out_sem.at[s])
        copy.start()
        return copy

    def temporal_grad(k, first, last):
        return nn(
            st[:, first * pixels:last * pixels], gext[first + k:last + k].reshape(-1, ch)
        )

    def spatial_grad(b, top, first, last):
        return nn(
            vt[:, first * pixels:last * pixels],
            hid[b, first:last, pl.ds(top, pixels)].reshape(-1, ch),
        )

    def lag_rows(k):
        return pl.ds(sw_rows + k * ch, ch)

    loads[1].wait()
    loads[0].wait()
    for s in range(early):
        hidden(s)
    loads[2].wait()
    for s in range(frames):
        st[:, s * pixels:(s + 1) * pixels] = sv[s].T
    for k in range(lags):
        part[lag_rows(k)] = temporal_grad(k, 0, frames - k)
    loads[3].wait()
    for s in range(frames):
        vt[:, s * pixels:(s + 1) * pixels] = vv[s].T
    for t in range(taps):
        part[t * ch:(t + 1) * ch] = spatial_grad(t % 3, 2 * width - (t // 3) * width, 0, early)

    for i in range(rim):
        @pl.when(fi < nf - 1)
        def _():
            halos[i].wait_recv()
        hidden(early + i)
        for k in range(i + 1, lags):
            part[lag_rows(k)] += temporal_grad(k, frames + i - k, frames + i - k + 1)
        if i < rim - 1:
            for t in range(taps):
                part[t * ch:(t + 1) * ch] += spatial_grad(
                    t % 3, 2 * width - (t // 3) * width, early + i, early + i + 1
                )

    def group_z(j):
        return lax.rem(zi + 1 + j, nz)

    def group_rows(j, owner_core):
        owner = group_z(j) * CORES + owner_core
        first = part[pl.ds(pl.multiple_of(owner * rw, math.gcd(rw, 256)), rw)]
        second = part[pl.ds(pl.multiple_of(sw_rows + owner * rt, math.gcd(rt, 256)), rt)]
        return jnp.concatenate([first, second], axis=0)

    def to_mate(j):
        s1[j] = group_rows(j, CORES - 1 - core).astype(BF16)
        copy = pltpu.make_async_remote_copy(
            src_ref=s1.at[j], dst_ref=r1.at[j], send_sem=send1.at[j], recv_sem=recv1.at[j],
            device_id={"frame": mate}, device_id_type=MESH,
        )
        copy.start()
        return copy

    lane = lax.broadcasted_iota(jnp.int32, (prow, lane_w), 1)
    copies1, copies2, copies3, stores = [], [], [], []

    def to_clips(j):
        copies1[j].wait_recv()
        total = group_rows(j, core) + r1[j].astype(F32)
        for d in range(nd):
            tile, off = (d * col) // lane_w, (d * col) % lane_w
            piece = None
            for q in range(fold):
                block = total[q * prow:(q + 1) * prow, tile * lane_w:(tile + 1) * lane_w]
                turn = (q * col - off) % lane_w
                if turn:
                    block = pltpu.roll(block, turn, 1)
                piece = block if piece is None else jnp.where(lane >= q * col, block, piece)
            s2[d, j] = piece.astype(BF16)
        for k in range(1, nd):
            to = lax.rem(di + k, nd)
            copy = pltpu.make_async_remote_copy(
                src_ref=s2.at[to, j], dst_ref=r2.at[k - 1, j],
                send_sem=send2.at[k - 1, j], recv_sem=recv2.at[k - 1, j],
                device_id={"dp": to}, device_id_type=MESH,
            )
            copy.start()
            copies2.append(copy)

    def to_owner(j):
        for k in range(nd - 1):
            copies2[j * (nd - 1) + k].wait_recv()
        total = s2[di, j].astype(F32)
        for k in range(nd - 1):
            total = total + r2[k, j].astype(F32)
        if j == nz - 1:
            own3[...] = total
        else:
            s3[j] = total.astype(BF16)
            copy = pltpu.make_async_remote_copy(
                src_ref=s3.at[j], dst_ref=r3.at[j], send_sem=send3.at[j], recv_sem=recv3.at[j],
                device_id={"frame": group_z(j) * CORES + core}, device_id_type=MESH,
            )
            copy.start()
            copies3.append(copy)

    first_tap = group_z(0) * CORES * rw // ch
    lead = max((z * CORES * rw) % ch for z in range(nz))
    for i in range(taps):
        t = lax.rem(first_tap + i, taps)
        top = pl.multiple_of(2 * width - (t // 3) * width, 16)
        spot = pl.ds(pl.multiple_of(t * ch, ch), ch)
        part[spot] += spatial_grad(lax.rem(t, 3), top, frames - 1, frames)
        while len(copies1) < nz and (
            i == taps - 1 or lead + (len(copies1) + 1) * CORES * rw <= (i + 1) * ch
        ):
            copies1.append(to_mate(len(copies1)))
            if len(copies1) > 1:
                to_clips(len(copies1) - 2)
    loads[4].wait()
    stores.append(grad_video(0))
    to_clips(nz - 1)
    for j in range(nz):
        if j + 1 < frames:
            stores.append(grad_video(j + 1))
        to_owner(j)
    for s in range(nz + 1, frames):
        stores.append(grad_video(s))

    total = own3[...]
    for j in range(nz - 1):
        copies3[j].wait_recv()
        total = total + r3[j].astype(F32)
    total = total * factor
    total = jnp.concatenate([total[:, q * col:(q + 1) * col] for q in range(fold)], axis=0)
    ows[...] = total[:rw].T
    owt[...] = total[rw:].T

    for copy in stores:
        copy.wait()
    for copy in copies1 + copies2 + copies3:
        copy.wait_send()

    @pl.when(fi > 0)
    def _():
        for halo in halos:
            halo.wait_send()


def place(gv, gs, gt, gv_out, gs_out, gt_out, gv_held, gs_held, gt_held, in_sem, out_sem):
    frames = gv.shape[0]
    hops = [(gv.at[s], gv_held.at[s], gv_out.at[s]) for s in range(frames)]
    hops += [(gs, gs_held, gs_out), (gt, gt_held, gt_out)]
    inward = [pltpu.make_async_copy(a, b, in_sem.at[i]) for i, (a, b, _) in enumerate(hops)]
    outward = [pltpu.make_async_copy(b, c, out_sem.at[i]) for i, (_, b, c) in enumerate(hops)]
    for copy in inward:
        copy.start()
    for first, second in zip(inward, outward):
        first.wait()
        second.start()
    for copy in outward:
        copy.wait()


def local(nd, nf, video, saved, grad_out, spatial_w, temporal_w):
    _, frames, height, width, ch = video.shape
    pixels = height * width
    nz = nf // CORES
    lags, taps = temporal_w.shape[0] // ch, spatial_w.shape[0] // ch
    rw, rt = spatial_w.shape[0] // nf, temporal_w.shape[0] // nf
    rows, col = rw + rt, ch // nd
    fold = max(1, LANES // col)
    prow, lane_w = rows // fold, col * fold
    slab = (frames, pixels, ch)
    factor = 1.0 / math.sqrt(float(nd * nf * frames * pixels))
    flops = 2 * frames * pixels * ch * ch * 2 * (lags + taps)
    anywhere = pl.BlockSpec(memory_space=pl.ANY)
    onchip = pl.BlockSpec(memory_space=pltpu.VMEM)
    dma = pltpu.SemaphoreType.DMA
    gv, gs, gt = pl.pallas_call(
        functools.partial(kernel, nd, nf, width, factor),
        out_shape=(
            jax.ShapeDtypeStruct(slab, BF16),
            jax.ShapeDtypeStruct((col, rw), F32),
            jax.ShapeDtypeStruct((col, rt), F32),
        ),
        in_specs=[anywhere] * 5,
        out_specs=(anywhere, onchip, onchip),
        scratch_shapes=[
            pltpu.VMEM((frames + lags - 1, pixels, ch), BF16),
            pltpu.VMEM(slab, BF16),
            pltpu.VMEM(slab, BF16),
            pltpu.VMEM(spatial_w.shape, BF16),
            pltpu.VMEM(temporal_w.shape, BF16),
            pltpu.VMEM((ch, frames * pixels), BF16),
            pltpu.VMEM((ch, frames * pixels), BF16),
            pltpu.VMEM((3, frames, pixels + 2 * width, ch), BF16),
            pltpu.VMEM((spatial_w.shape[0] + temporal_w.shape[0], ch), F32),
            pltpu.VMEM(slab, BF16),
            pltpu.VMEM((nz, rows, ch), BF16),
            pltpu.VMEM((nz, rows, ch), BF16),
            pltpu.VMEM((nd, nz, prow, lane_w), BF16),
            pltpu.VMEM((nd - 1, nz, prow, lane_w), BF16),
            pltpu.VMEM((nz - 1, prow, lane_w), BF16),
            pltpu.VMEM((nz - 1, prow, lane_w), BF16),
            pltpu.VMEM((prow, lane_w), F32),
            dma((5,)),
            dma((frames,)),
            dma((lags - 1,)),
            dma((lags - 1,)),
            dma((nz,)),
            dma((nz,)),
            dma((nd - 1, nz)),
            dma((nd - 1, nz)),
            dma((nz - 1,)),
            dma((nz - 1,)),
        ],
        compiler_params=pltpu.CompilerParams(
            collective_id=0, has_side_effects=True, vmem_limit_bytes=VMEM_BYTES
        ),
        cost_estimate=pl.CostEstimate(
            flops=flops, bytes_accessed=8 * frames * pixels * ch, transcendentals=0
        ),
        name="conv_backward",
    )(
        grad_out.reshape(slab), saved.reshape(slab), video.reshape(slab), spatial_w, temporal_w
    )
    gv, gs, gt = pl.pallas_call(
        place,
        out_shape=tuple(jax.ShapeDtypeStruct(x.shape, x.dtype) for x in (gv, gs, gt)),
        in_specs=[anywhere] * 3,
        out_specs=(anywhere,) * 3,
        scratch_shapes=[pltpu.VMEM(x.shape, x.dtype) for x in (gv, gs, gt)]
        + [dma((frames + 2,)), dma((frames + 2,))],
        compiler_params=pltpu.CompilerParams(vmem_limit_bytes=VMEM_BYTES),
        name="place_results",
    )(gv, gs, gt)
    return (gv.reshape(video.shape), gs.T, gt.T)


def solution(mesh):
    nd, nf = mesh.shape["dp"], mesh.shape["frame"]
    return jax.shard_map(
        functools.partial(local, nd, nf),
        mesh=mesh,
        in_specs=(
            P("dp", "frame", None, None, None),
            P("dp", "frame", None, None, None),
            P("dp", "frame", None, None, None),
            P(),
            P(),
        ),
        out_specs=(P("dp", "frame", None, None, None), P("frame", "dp"), P("frame", "dp")),
        check_vma=False,
    )
```

```python
import functools
import math

import jax
import jax.numpy as jnp
from jax import lax
from jax.experimental import pallas as pl
from jax.experimental.pallas import tpu as pltpu
from jax.sharding import PartitionSpec as P

F32 = jnp.float32
BF16 = jnp.bfloat16
MESH = pl.DeviceIdType.MESH
LANES = 128
CORES = 2
VMEM_BYTES = 60 * 1024 * 1024


def nt(lhs, rhs):
    return lax.dot_general(lhs, rhs, (((1,), (1,)), ((), ())), preferred_element_type=F32)


def nn(lhs, rhs):
    return lax.dot_general(lhs, rhs, (((1,), (0,)), ((), ())), preferred_element_type=F32)


def kernel(
    nd, nf, width, factor,
    g_hbm, s_hbm, v_hbm, sw_hbm, tw_hbm,
    gv_hbm, ows, owt,
    gext, sv, vv, sw, tw, st, vt, hid, part, gv, s1, r1, s2, r2, s3, r3, own3,
    in_sem, out_sem, halo_send, halo_recv, send1, recv1, send2, recv2, send3, recv3,
):
    nz = nf // CORES
    frames, pixels, ch = v_hbm.shape
    lags = tw_hbm.shape[0] // ch
    taps = sw_hbm.shape[0] // ch
    rim = lags - 1
    early = frames - rim
    sw_rows = sw_hbm.shape[0]
    rw, rt = sw_rows // nf, tw_hbm.shape[0] // nf
    rows = rw + rt
    col = ch // nd
    fold = max(1, LANES // col)
    lane_w = col * fold
    prow = rows // fold

    di, fi = lax.axis_index("dp"), lax.axis_index("frame")
    core, zi = lax.rem(fi, CORES), fi // CORES
    mate = zi * CORES + (CORES - 1 - core)

    loads = []
    for i, (src, dst) in enumerate(
        ((g_hbm, gext.at[pl.ds(0, frames)]), (tw_hbm, tw), (s_hbm, sv), (v_hbm, vv), (sw_hbm, sw))
    ):
        copy = pltpu.make_async_copy(src, dst, in_sem.at[i])
        copy.start()
        loads.append(copy)

    barrier = pltpu.get_barrier_semaphore()
    greeted = [{"frame": mate}, {"frame": lax.rem(fi + 1, nf)}, {"frame": lax.rem(fi + nf - 1, nf)}]
    greeted += [{"dp": lax.rem(di + k, nd)} for k in range(1, nd)]
    greeted += [{"frame": lax.rem(zi + k, nz) * CORES + core} for k in range(1, nz)]
    for device in greeted:
        pl.semaphore_signal(barrier, inc=1, device_id=device, device_id_type=MESH)
    pl.semaphore_wait(barrier, len(greeted))

    halos = [
        pltpu.make_async_remote_copy(
            src_ref=g_hbm.at[i], dst_ref=gext.at[frames + i],
            send_sem=halo_send.at[i], recv_sem=halo_recv.at[i],
            device_id={"frame": lax.rem(fi + nf - 1, nf)}, device_id_type=MESH,
        )
        for i in range(rim)
    ]

    @pl.when(fi > 0)
    def _():
        for halo in halos:
            halo.start()

    @pl.when(fi == nf - 1)
    def _():
        gext[frames:] = jnp.zeros((rim, pixels, ch), BF16)

    blank = jnp.zeros((3, frames, width, ch), BF16)
    hid[:, :, :width] = blank
    hid[:, :, width + pixels:] = blank

    column = lax.rem(lax.broadcasted_iota(jnp.int32, (pixels, ch), 0), width)

    def hidden(s):
        later = jnp.concatenate([gext[s + k] for k in range(lags)], axis=1)
        weight = jnp.concatenate([tw[k * ch:(k + 1) * ch] for k in range(lags)], axis=1)
        value = nt(later, weight)
        for b in (-1, 0, 1):
            moved = value
            if b == 1:
                moved = jnp.where(column >= 1, pltpu.roll(value, 1, 0), 0.0)
            if b == -1:
                moved = jnp.where(column < width - 1, pltpu.roll(value, pixels - 1, 0), 0.0)
            hid[b + 1, s, width:width + pixels] = moved.astype(BF16)

    def moved_rows(a):
        return pl.ds(width - a * width, pixels)

    def grad_video(s):
        moved = jnp.concatenate(
            [hid[b + 1, s, moved_rows(a)] for a in (-1, 0, 1) for b in (-1, 0, 1)], axis=1
        )
        weight = jnp.concatenate([sw[t * ch:(t + 1) * ch] for t in range(taps)], axis=1)
        gv[s] = nt(moved, weight).astype(BF16)
        copy = pltpu.make_async_copy(gv.at[s], gv_hbm.at[s], out_sem.at[s])
        copy.start()
        return copy

    def temporal_grad(k, first, last):
        return nn(
            st[:, first * pixels:last * pixels], gext[first + k:last + k].reshape(-1, ch)
        )

    def spatial_grad(b, top, first, last):
        return nn(
            vt[:, first * pixels:last * pixels],
            hid[b, first:last, pl.ds(top, pixels)].reshape(-1, ch),
        )

    def lag_rows(k):
        return pl.ds(sw_rows + k * ch, ch)

    loads[1].wait()
    loads[0].wait()
    for s in range(early):
        hidden(s)
    loads[2].wait()
    for s in range(frames):
        st[:, s * pixels:(s + 1) * pixels] = sv[s].T
    for k in range(lags):
        part[lag_rows(k)] = temporal_grad(k, 0, frames - k)
    loads[3].wait()
    for s in range(frames):
        vt[:, s * pixels:(s + 1) * pixels] = vv[s].T
    for t in range(taps):
        part[t * ch:(t + 1) * ch] = spatial_grad(t % 3, 2 * width - (t // 3) * width, 0, early)

    for i in range(rim):
        @pl.when(fi < nf - 1)
        def _():
            halos[i].wait_recv()
        hidden(early + i)
        for k in range(i + 1, lags):
            part[lag_rows(k)] += temporal_grad(k, frames + i - k, frames + i - k + 1)
        if i < rim - 1:
            for t in range(taps):
                part[t * ch:(t + 1) * ch] += spatial_grad(
                    t % 3, 2 * width - (t // 3) * width, early + i, early + i + 1
                )

    def group_z(j):
        return lax.rem(zi + 1 + j, nz)

    def group_rows(j, owner_core):
        owner = group_z(j) * CORES + owner_core
        first = part[pl.ds(pl.multiple_of(owner * rw, math.gcd(rw, 256)), rw)]
        second = part[pl.ds(pl.multiple_of(sw_rows + owner * rt, math.gcd(rt, 256)), rt)]
        return jnp.concatenate([first, second], axis=0)

    def to_mate(j):
        s1[j] = group_rows(j, CORES - 1 - core).astype(BF16)
        copy = pltpu.make_async_remote_copy(
            src_ref=s1.at[j], dst_ref=r1.at[j], send_sem=send1.at[j], recv_sem=recv1.at[j],
            device_id={"frame": mate}, device_id_type=MESH,
        )
        copy.start()
        return copy

    lane = lax.broadcasted_iota(jnp.int32, (prow, lane_w), 1)
    copies1, copies2, copies3, stores = [], [], [], []

    def to_clips(j):
        copies1[j].wait_recv()
        total = group_rows(j, core) + r1[j].astype(F32)
        for d in range(nd):
            tile, off = (d * col) // lane_w, (d * col) % lane_w
            piece = None
            for q in range(fold):
                block = total[q * prow:(q + 1) * prow, tile * lane_w:(tile + 1) * lane_w]
                turn = (q * col - off) % lane_w
                if turn:
                    block = pltpu.roll(block, turn, 1)
                piece = block if piece is None else jnp.where(lane >= q * col, block, piece)
            s2[d, j] = piece.astype(BF16)
        for k in range(1, nd):
            to = lax.rem(di + k, nd)
            copy = pltpu.make_async_remote_copy(
                src_ref=s2.at[to, j], dst_ref=r2.at[k - 1, j],
                send_sem=send2.at[k - 1, j], recv_sem=recv2.at[k - 1, j],
                device_id={"dp": to}, device_id_type=MESH,
            )
            copy.start()
            copies2.append(copy)

    def to_owner(j):
        for k in range(nd - 1):
            copies2[j * (nd - 1) + k].wait_recv()
        total = s2[di, j].astype(F32)
        for k in range(nd - 1):
            total = total + r2[k, j].astype(F32)
        if j == nz - 1:
            own3[...] = total
        else:
            s3[j] = total.astype(BF16)
            copy = pltpu.make_async_remote_copy(
                src_ref=s3.at[j], dst_ref=r3.at[j], send_sem=send3.at[j], recv_sem=recv3.at[j],
                device_id={"frame": group_z(j) * CORES + core}, device_id_type=MESH,
            )
            copy.start()
            copies3.append(copy)

    first_tap = group_z(0) * CORES * rw // ch
    lead = max((z * CORES * rw) % ch for z in range(nz))
    for i in range(taps):
        t = lax.rem(first_tap + i, taps)
        top = pl.multiple_of(2 * width - (t // 3) * width, 16)
        spot = pl.ds(pl.multiple_of(t * ch, ch), ch)
        part[spot] += spatial_grad(lax.rem(t, 3), top, frames - 1, frames)
        while len(copies1) < nz and (
            i == taps - 1 or lead + (len(copies1) + 1) * CORES * rw <= (i + 1) * ch
        ):
            copies1.append(to_mate(len(copies1)))
            if len(copies1) > 1:
                to_clips(len(copies1) - 2)
    loads[4].wait()
    stores.append(grad_video(0))
    to_clips(nz - 1)
    for j in range(nz):
        if j + 1 < frames and j != nz - 2:
            stores.append(grad_video(j + 1))
        to_owner(j)
        if j + 1 < frames and j == nz - 2:
            stores.append(grad_video(j + 1))
    for s in range(nz + 1, frames):
        stores.append(grad_video(s))

    total = own3[...]
    for j in range(nz - 1):
        copies3[j].wait_recv()
        total = total + r3[j].astype(F32)
    total = total * factor
    total = jnp.concatenate([total[:, q * col:(q + 1) * col] for q in range(fold)], axis=0)
    ows[...] = total[:rw].T
    owt[...] = total[rw:].T

    for copy in stores:
        copy.wait()
    for copy in copies1 + copies2 + copies3:
        copy.wait_send()

    @pl.when(fi > 0)
    def _():
        for halo in halos:
            halo.wait_send()


def place(gv, gs, gt, gv_out, gs_out, gt_out, gv_held, gs_held, gt_held, in_sem, out_sem):
    frames = gv.shape[0]
    hops = [(gv.at[s], gv_held.at[s], gv_out.at[s]) for s in range(frames)]
    hops += [(gs, gs_held, gs_out), (gt, gt_held, gt_out)]
    inward = [pltpu.make_async_copy(a, b, in_sem.at[i]) for i, (a, b, _) in enumerate(hops)]
    outward = [pltpu.make_async_copy(b, c, out_sem.at[i]) for i, (_, b, c) in enumerate(hops)]
    for copy in inward:
        copy.start()
    for first, second in zip(inward, outward):
        first.wait()
        second.start()
    for copy in outward:
        copy.wait()


def local(nd, nf, video, saved, grad_out, spatial_w, temporal_w):
    _, frames, height, width, ch = video.shape
    pixels = height * width
    nz = nf // CORES
    lags, taps = temporal_w.shape[0] // ch, spatial_w.shape[0] // ch
    rw, rt = spatial_w.shape[0] // nf, temporal_w.shape[0] // nf
    rows, col = rw + rt, ch // nd
    fold = max(1, LANES // col)
    prow, lane_w = rows // fold, col * fold
    slab = (frames, pixels, ch)
    factor = 1.0 / math.sqrt(float(nd * nf * frames * pixels))
    flops = 2 * frames * pixels * ch * ch * 2 * (lags + taps)
    anywhere = pl.BlockSpec(memory_space=pl.ANY)
    onchip = pl.BlockSpec(memory_space=pltpu.VMEM)
    dma = pltpu.SemaphoreType.DMA
    gv, gs, gt = pl.pallas_call(
        functools.partial(kernel, nd, nf, width, factor),
        out_shape=(
            jax.ShapeDtypeStruct(slab, BF16),
            jax.ShapeDtypeStruct((col, rw), F32),
            jax.ShapeDtypeStruct((col, rt), F32),
        ),
        in_specs=[anywhere] * 5,
        out_specs=(anywhere, onchip, onchip),
        scratch_shapes=[
            pltpu.VMEM((frames + lags - 1, pixels, ch), BF16),
            pltpu.VMEM(slab, BF16),
            pltpu.VMEM(slab, BF16),
            pltpu.VMEM(spatial_w.shape, BF16),
            pltpu.VMEM(temporal_w.shape, BF16),
            pltpu.VMEM((ch, frames * pixels), BF16),
            pltpu.VMEM((ch, frames * pixels), BF16),
            pltpu.VMEM((3, frames, pixels + 2 * width, ch), BF16),
            pltpu.VMEM((spatial_w.shape[0] + temporal_w.shape[0], ch), F32),
            pltpu.VMEM(slab, BF16),
            pltpu.VMEM((nz, rows, ch), BF16),
            pltpu.VMEM((nz, rows, ch), BF16),
            pltpu.VMEM((nd, nz, prow, lane_w), BF16),
            pltpu.VMEM((nd - 1, nz, prow, lane_w), BF16),
            pltpu.VMEM((nz - 1, prow, lane_w), BF16),
            pltpu.VMEM((nz - 1, prow, lane_w), BF16),
            pltpu.VMEM((prow, lane_w), F32),
            dma((5,)),
            dma((frames,)),
            dma((lags - 1,)),
            dma((lags - 1,)),
            dma((nz,)),
            dma((nz,)),
            dma((nd - 1, nz)),
            dma((nd - 1, nz)),
            dma((nz - 1,)),
            dma((nz - 1,)),
        ],
        compiler_params=pltpu.CompilerParams(
            collective_id=0, has_side_effects=True, vmem_limit_bytes=VMEM_BYTES
        ),
        cost_estimate=pl.CostEstimate(
            flops=flops, bytes_accessed=8 * frames * pixels * ch, transcendentals=0
        ),
        name="conv_backward",
    )(
        grad_out.reshape(slab), saved.reshape(slab), video.reshape(slab), spatial_w, temporal_w
    )
    gv, gs, gt = pl.pallas_call(
        place,
        out_shape=tuple(jax.ShapeDtypeStruct(x.shape, x.dtype) for x in (gv, gs, gt)),
        in_specs=[anywhere] * 3,
        out_specs=(anywhere,) * 3,
        scratch_shapes=[pltpu.VMEM(x.shape, x.dtype) for x in (gv, gs, gt)]
        + [dma((frames + 2,)), dma((frames + 2,))],
        compiler_params=pltpu.CompilerParams(vmem_limit_bytes=VMEM_BYTES),
        name="place_results",
    )(gv, gs, gt)
    return (gv.reshape(video.shape), gs.T, gt.T)


def solution(mesh):
    nd, nf = mesh.shape["dp"], mesh.shape["frame"]
    return jax.shard_map(
        functools.partial(local, nd, nf),
        mesh=mesh,
        in_specs=(
            P("dp", "frame", None, None, None),
            P("dp", "frame", None, None, None),
            P("dp", "frame", None, None, None),
            P(),
            P(),
        ),
        out_specs=(P("dp", "frame", None, None, None), P("frame", "dp"), P("frame", "dp")),
        check_vma=False,
    )
```
